512 devices in a mesh: dp: 32 (over z, core), ctx: 16 (over y, x).
Axes of the slice: x: 4, y: 4, z: 16, core: 2. Of those that a mesh axis runs over, the one named last changes fastest.
Arguments:
- queries: bfloat16 [4, 64, 128, 576], P(None, 'dp', 'ctx'), may hold values from -14 to 14
- latent_cache: bfloat16 [64, 24576, 576], P('dp', 'ctx'), may hold values from -7 to 7
- new_latent: bfloat16 [4, 64, 576], P(None, 'dp'), may hold values from -12 to 12
- lengths: int32 [64], P('dp'), may hold values from 3072 to 24576, as said below
- value_up: bfloat16 [128, 512, 128], P('ctx', 'dp'), may hold values from -0.25 to 0.25
Outputs:
- attended: float32 [4, 64, 128, 128], P(None, 'dp', 'ctx')
The draws below stay inside these ranges and needn't reach their ends.
Inputs may be any that keep to these rules, and one draw needn't show every extreme that they name: Row b's cache holds live entries at positions 0 to lengths[b] - 1 and some row's length is 24576 in every draw.
All inputs are finite; a program needn't handle non-finite values.
Results may differ from the reference program's by a relative error of at most 0.006.
Values may be sent and summed in bfloat16 or wider, within the bound.
No kernel may reach another device: no remote copies, remote signals or barrier semaphores. Data moves between devices by JAX's collectives and lax.ppermute only.
A program may use at most 64 MiB of HBM per device.

```python
import jax
import jax.numpy as jnp
from jax import lax

H = 128
LAT = 512
ROPE = 64
NOPE = 128
VDIM = 128
STEPS = 4
ROWS = 64
CTX_LEN = 24576


def draw_queries(key, part):
    key = jax.random.fold_in(key, 11)
    normal_key = jax.random.fold_in(key, 0)
    values = 2.0 * jnp.clip(jax.random.normal(normal_key, (STEPS, ROWS, H, LAT + ROPE), jnp.float32), -6.0, 6.0)
    return values.astype(jnp.bfloat16)


def draw_latent_cache(key, part):
    key = jax.random.fold_in(key, 12)
    normal_key = jax.random.fold_in(key, 0)
    values = jnp.clip(jax.random.normal(normal_key, (ROWS, CTX_LEN, LAT + ROPE), jnp.float32), -6.0, 6.0)
    return values.astype(jnp.bfloat16)


def draw_lengths(key, part):
    key = jax.random.fold_in(key, 13)
    length_key, chosen_key = jax.random.split(key)
    drawn = jax.random.randint(length_key, (ROWS,), CTX_LEN // 8, CTX_LEN + 1, jnp.int32)
    chosen = jax.random.randint(chosen_key, (), 0, ROWS, jnp.int32)
    row_index = jnp.arange(ROWS, dtype=jnp.int32)
    return jnp.where(row_index == chosen, CTX_LEN, drawn).astype(jnp.int32)


def block_scale(rng, dims, cuts, least, largest):
    factor_of = 1.0
    for position, shards_of in cuts:
        steps = jax.random.uniform(jax.random.fold_in(jax.random.fold_in(rng, 6), position), (shards_of,), jnp.float32, least / len(cuts), largest / len(cuts))
        factor_of = factor_of * jnp.repeat(jnp.exp(steps), dims[position] // shards_of).reshape((-1,) + (1,) * (len(dims) - 1 - position))
    return factor_of


def centred(own_key, extent, width, bound, pieces=(), kind=jnp.bfloat16):
    values = jax.random.normal(own_key, extent, jnp.float32) * width
    if len(pieces) > 0:
        values = block_scale(own_key, extent, pieces, -0.22, 0.18) * values
    return jnp.clip(values, min=-bound, max=bound).astype(kind)


def setup_inputs(seed: int = 0) -> dict:
    key_list = jax.random.split(jax.random.key(seed), 6)
    return {
        "queries": draw_queries(jax.random.fold_in(key_list[5], 71), 0),
        "latent_cache": draw_latent_cache(jax.random.fold_in(key_list[5], 71), 0),
        "new_latent": centred(key_list[2], (STEPS, ROWS, LAT + ROPE), 3.0, 12.0, ((1, 32),)),
        "lengths": draw_lengths(jax.random.fold_in(key_list[5], 71), 0),
        "value_up": centred(key_list[4], (H, LAT, VDIM), LAT ** -0.5, 0.25, ((0, 16), (1, 32))),
    }


def rotate(values, positions):
    half_width = values.shape[-1] // 2
    pair_index = jnp.arange(half_width, dtype=jnp.float32)
    frequency = jnp.power(jnp.float32(10000.0), -2.0 * pair_index / values.shape[-1])
    angles = positions.astype(jnp.float32)[..., None] * frequency
    first_half = values[..., :half_width].astype(jnp.float32)
    second_half = values[..., half_width:].astype(jnp.float32)
    cosine = jnp.cos(angles)
    sine_part = jnp.sin(angles)
    return jnp.concatenate([first_half * cosine - second_half * sine_part, first_half * sine_part + second_half * cosine], axis=-1)


def reference(queries, latent_cache, new_latent, lengths, value_up):
    step_ids = jnp.arange(STEPS, dtype=jnp.int32)
    positions = lengths[None, :] + step_ids[:, None]
    query_ready = jnp.concatenate([queries[..., :LAT], rotate(queries[..., LAT:], positions[:, :, None]).astype(jnp.bfloat16)], axis=-1)
    new_ready = jnp.concatenate([new_latent[..., :LAT], rotate(new_latent[..., LAT:], positions).astype(jnp.bfloat16)], axis=-1)
    score_scale = (NOPE + ROPE) ** -0.5
    slot_ids = jnp.arange(CTX_LEN, dtype=jnp.int32)
    own_mask = step_ids[None, :] <= step_ids[:, None]

    def attend_row(items):
        query_row, cache_row, new_row, length = items
        key_rows = jnp.concatenate([cache_row, new_row], axis=0)
        scores = jnp.einsum("shc,kc->shk", query_row.astype(jnp.float32), key_rows.astype(jnp.float32)) * score_scale
        valid_mask = jnp.concatenate([jnp.broadcast_to(slot_ids < length, (STEPS, CTX_LEN)), own_mask], axis=1)[:, None, :]
        row_top = jnp.max(jnp.where(valid_mask, scores, -1e30), axis=-1, keepdims=True)
        weights = jnp.where(valid_mask, jnp.exp(scores - row_top), 0.0)
        weight_sum = jnp.sum(weights, axis=-1, keepdims=True)
        weights_low = lax.optimization_barrier(weights.astype(jnp.bfloat16))
        mixed = jnp.einsum("shk,kl->shl", weights_low.astype(jnp.float32), key_rows[:, :LAT].astype(jnp.float32))
        return (mixed / weight_sum).astype(jnp.bfloat16)

    latent_out = lax.map(attend_row, (jnp.swapaxes(query_ready, 0, 1), latent_cache, jnp.swapaxes(new_ready, 0, 1), lengths))
    latent_out = lax.optimization_barrier(latent_out)
    attended = jnp.einsum("bshl,hlv->sbhv", latent_out.astype(jnp.float32), value_up.astype(jnp.float32))
    return attended.astype(jnp.float32)
```

```python
import jax
import jax.numpy as jnp
from jax import lax
from jax.experimental import pallas as pl
from jax.experimental.pallas import tpu as pltpu
from jax.sharding import PartitionSpec as P

LAT = 512
ROPE = 64
HALF = 32
NOPE = 128
SCALE = (NOPE + ROPE) ** (-0.5)
LOG2E = 1.4426950408889634
FLOOR = -1e30
F32 = jnp.float32
BF16 = jnp.bfloat16
NT = (((1,), (1,)), ((), ()))


def vmem():
    return pl.BlockSpec(memory_space=pltpu.VMEM)


def smem():
    return pl.BlockSpec(memory_space=pltpu.SMEM)


def swap_halves(x):
    lane = lax.broadcasted_iota(jnp.int32, x.shape, x.ndim - 1)
    width = x.shape[-1]
    ahead = pltpu.roll(x, width - HALF, x.ndim - 1)
    behind = pltpu.roll(x, HALF, x.ndim - 1)
    return jnp.where(lane % ROPE < HALF, ahead, behind)


def pack_kernel(q_ref, out_ref):
    steps, rows, heads, _ = q_ref.shape
    parts = []
    rotary = []
    for r in range(rows):
        for s in range(steps):
            block = q_ref[s, r].astype(F32)
            parts.append(block[:, :LAT])
            rotary.append(block[:, LAT:])
    parts.append(jnp.concatenate(rotary, axis=1))
    whole = jnp.concatenate(parts, axis=0).astype(BF16)
    for d in range(out_ref.shape[0]):
        out_ref[d] = whole


def pack_queries(queries, shards):
    steps, rows, heads, _ = queries.shape
    count = steps * rows * heads
    return pl.pallas_call(
        pack_kernel,
        out_shape=jax.ShapeDtypeStruct((shards, count + heads, LAT), BF16),
        in_specs=[vmem()],
        out_specs=vmem(),
        name="pack_queries",
    )(queries)


def fresh_kernel(q_ref, new_ref, cos_ref, sin_ref, mixed_ref, lse_ref):
    steps, rows, heads, _ = q_ref.shape
    count = rows * steps * heads
    keys = rows * steps
    cos = cos_ref[...]
    sin = sin_ref[...]
    q_lat = []
    q_rot = []
    key_lat = []
    key_rot = []
    for r in range(rows):
        for s in range(steps):
            row_cos = cos[r * steps + s : r * steps + s + 1]
            row_sin = sin[r * steps + s : r * steps + s + 1]
            block = q_ref[s, r].astype(F32)
            q_lat.append(block[:, :LAT])
            wide = jnp.concatenate([block[:, LAT:], block[:, LAT:]], axis=1)
            q_rot.append(wide * row_cos + swap_halves(wide) * row_sin)
            key = new_ref[s, r : r + 1].astype(F32)
            key_lat.append(key[:, :LAT])
            wide = jnp.concatenate([key[:, LAT:], key[:, LAT:]], axis=1)
            wide = jnp.broadcast_to(wide, (8, 2 * ROPE))
            wide = wide * row_cos + swap_halves(wide) * row_sin
            key_rot.append(wide[:1])
    q_lat = jnp.concatenate(q_lat, axis=0).astype(BF16)
    q_rot = jnp.concatenate(q_rot, axis=0)[:, :ROPE].astype(BF16)
    pad = jnp.zeros((128 - keys, LAT), F32)
    key_lat = jnp.concatenate(key_lat + [pad], axis=0).astype(BF16)
    key_rot = jnp.concatenate(key_rot + [pad[:, : 2 * ROPE]], axis=0)[:, :ROPE].astype(BF16)
    scores = lax.dot_general(q_lat, key_lat, NT, preferred_element_type=F32)
    scores += lax.dot_general(q_rot, key_rot, NT, preferred_element_type=F32)
    scores *= SCALE
    query = lax.broadcasted_iota(jnp.int32, (count, 128), 0) // heads
    key = lax.broadcasted_iota(jnp.int32, (count, 128), 1)
    valid = (key <= query) & (key // steps == query // steps)
    scores = jnp.where(valid, scores, FLOOR)
    top = jnp.max(scores, axis=1, keepdims=True)
    weights = jnp.where(valid, jnp.exp(scores - top), 0.0)
    total = jnp.sum(weights, axis=1, keepdims=True)
    mixed = jnp.dot(weights.astype(BF16), key_lat, preferred_element_type=F32)
    mixed_ref[...] = mixed / total
    lse_ref[...] = as_rows((top + jnp.log(total)).reshape(rows, steps * heads, 1))


def as_rows(column):
    n, span, _ = column.shape
    row = lax.broadcasted_iota(jnp.int32, (n, span, 128), 1)
    lane = lax.broadcasted_iota(jnp.int32, (n, span, 128), 2)
    return jnp.sum(jnp.where(row == lane, column, 0.0), axis=1)


def fresh_part(queries, new_latent, cos, sin):
    steps, rows, heads, _ = queries.shape
    count = steps * rows * heads
    return pl.pallas_call(
        fresh_kernel,
        out_shape=(
            jax.ShapeDtypeStruct((count, LAT), F32),
            jax.ShapeDtypeStruct((rows, 128), F32),
        ),
        in_specs=[vmem()] * 4,
        out_specs=(vmem(), vmem()),
        name="fresh_part",
    )(queries, new_latent, cos, sin)


def attend_kernel(live_ref, q_ref, cos_ref, sin_ref, cache_ref, out_ref, keys, q_scr, sems):
    rows, span, _ = cache_ref.shape
    shards, stride, _ = q_ref.shape
    heads = 8
    count = stride - heads
    per_row = count // rows
    steps = per_row // heads
    copies = [
        pltpu.make_async_copy(cache_ref.at[r], keys.at[r], sems.at[r]) for r in range(rows)
    ]
    for copy in copies:
        copy.start()
    packed = q_ref[:, count:, :].astype(F32).reshape(shards * heads, LAT)
    lse_rows = []
    for r in range(rows):
        q_scr[:, :LAT] = q_ref[:, r * per_row : (r + 1) * per_row, :].reshape(
            shards * per_row, LAT
        )
        width = steps * ROPE
        part = packed[:, r * width : (r + 1) * width]
        turned = part * cos_ref[r : r + 1] + swap_halves(part) * sin_ref[r : r + 1]
        turned = jnp.stack(
            [
                turned[:, s * ROPE : (s + 1) * ROPE].reshape(shards, heads, ROPE)
                for s in range(steps)
            ],
            axis=1,
        ).reshape(shards * per_row, ROPE)
        q_scr[:, LAT:] = turned.astype(BF16)
        copies[r].wait()
        scores = lax.dot_general(q_scr[...], keys[r], NT, preferred_element_type=F32)
        slot = lax.broadcasted_iota(jnp.int32, scores.shape, 1)
        scores = jnp.where(slot < live_ref[r], scores, FLOOR)
        top = jnp.max(scores, axis=1, keepdims=True)
        weights = jnp.exp2((scores - top) * (SCALE * LOG2E))
        total = jnp.sum(weights, axis=1, keepdims=True)
        mixed = jnp.dot(weights.astype(BF16), keys[r, :, :LAT], preferred_element_type=F32)
        mixed = mixed * (1.0 / total)
        out_ref[:, r * per_row : (r + 1) * per_row, :] = (
            mixed.astype(BF16).reshape(shards, per_row, LAT)
        )
        lse = jnp.where(live_ref[r] > 0, top * SCALE + jnp.log(total), FLOOR)
        lse_rows.append(as_rows(lse.reshape(shards, per_row, 1)))
    tail = jnp.zeros((shards, heads, 128), F32)
    which = lax.broadcasted_iota(jnp.int32, tail.shape, 1)
    for r in range(rows):
        rest = lse_rows[r]
        for term in range(3):
            piece = rest.astype(BF16).astype(F32)
            tail = jnp.where(which == 3 * r + term, piece[:, None, :], tail)
            rest = rest - piece
    tail = jnp.concatenate([tail, jnp.zeros((shards, heads, LAT - 128), F32)], axis=2)
    out_ref[:, count:, :] = tail.astype(BF16)


def attend(live, gathered, cos, sin, cache):
    rows, span, width = cache.shape
    shards, stride, _ = gathered.shape
    per_row = (stride - 8) // rows
    return pl.pallas_call(
        attend_kernel,
        out_shape=jax.ShapeDtypeStruct(gathered.shape, BF16),
        in_specs=[smem(), vmem(), vmem(), vmem(), pl.BlockSpec(memory_space=pl.ANY)],
        out_specs=vmem(),
        scratch_shapes=[
            pltpu.VMEM((rows, span, width), BF16),
            pltpu.VMEM((shards * per_row, width), BF16),
            pltpu.SemaphoreType.DMA((rows,)),
        ],
        compiler_params=pltpu.CompilerParams(vmem_limit_bytes=40 * 1024 * 1024),
        cost_estimate=pl.CostEstimate(
            flops=2 * rows * shards * per_row * span * (width + LAT),
            bytes_accessed=cache.size * 2 + gathered.size * 4,
            transcendentals=rows * shards * per_row * span,
        ),
        name="attend",
    )(live, gathered, cos, sin, cache)


def merge_kernel(place_ref, got_ref, fresh_ref, fresh_lse_ref, own_ref, other_ref, out_ref, up):
    shards, stride, _ = got_ref.shape
    steps, rows, heads, _ = out_ref.shape
    count = stride - heads
    per_row = count // rows
    blocks, _, depth, _ = own_ref.shape
    for source, ref in enumerate((own_ref, other_ref)):
        for b in range(blocks):
            start = pl.multiple_of(place_ref[source * blocks + b] * depth, depth)
            up[:, pl.ds(start, depth), :] = ref[b]
    tail = got_ref[:, count:, :128].astype(F32)
    sub = lax.broadcasted_iota(jnp.int32, (per_row, 128), 0)
    lane = lax.broadcasted_iota(jnp.int32, (per_row, 128), 1)
    eye = sub == lane

    def column(row):
        return jnp.sum(jnp.where(eye, row, 0.0), axis=1, keepdims=True)

    merged = []
    for r in range(rows):
        spread = tail[:, 3 * r] + tail[:, 3 * r + 1] + tail[:, 3 * r + 2]
        own = fresh_lse_ref[r : r + 1]
        top = jnp.maximum(jnp.max(spread, axis=0, keepdims=True), own)
        factor = jnp.exp(spread - top)
        own_factor = jnp.exp(own - top)
        scale = 1.0 / (jnp.sum(factor, axis=0, keepdims=True) + own_factor)
        factor = factor * scale
        first = r * per_row
        total = column(own_factor * scale) * fresh_ref[first : first + per_row]
        for d in range(shards):
            piece = got_ref[d, first : first + per_row, :].astype(F32)
            total += column(factor[d : d + 1]) * piece
        merged.append(total)
    latent = jnp.concatenate(merged, axis=0).astype(BF16)
    head = lax.broadcasted_iota(jnp.int32, (count, 128), 0) % heads
    result = jnp.zeros((count, 128), F32)
    for h in range(heads):
        product = jnp.dot(latent, up[h], preferred_element_type=F32)
        result = jnp.where(head == h, product, result)
    for r in range(rows):
        for s in range(steps):
            first = (r * steps + s) * heads
            out_ref[s, r] = result[first : first + heads]


def merge(place, got, fresh, fresh_lse, own, other, steps, rows):
    blocks, heads, depth, width = own.shape
    return pl.pallas_call(
        merge_kernel,
        out_shape=jax.ShapeDtypeStruct((steps, rows, heads, width), F32),
        in_specs=[smem()] + [vmem()] * 5,
        out_specs=vmem(),
        scratch_shapes=[pltpu.VMEM((heads, 2 * blocks * depth, width), BF16)],
        compiler_params=pltpu.CompilerParams(vmem_limit_bytes=16 * 1024 * 1024),
        name="merge",
    )(place, got, fresh, fresh_lse, own, other)


def body(queries, latent_cache, new_latent, lengths, value_up):
    steps, rows, heads, _ = queries.shape
    shards = lax.axis_size("ctx")
    lines = lax.axis_size("dp")
    chips = lines // 2
    span = latent_cache.shape[1]

    def from_line(x, reach):
        pairs = []
        for line in range(lines):
            z, core = line // 2, line % 2
            sign = 1 - 2 * core
            pairs.append((((z + sign * reach) % chips) * 2 + core, line))
        return lax.ppermute(x, "dp", pairs)

    packed = pack_queries(queries, shards)
    gathered = lax.all_to_all(packed, "ctx", 0, 0, tiled=True)

    held = value_up[None]
    reach = chips // 2
    while reach >= 1:
        held = jnp.concatenate([held, from_line(held, reach)], axis=0)
        reach //= 2
    other = lax.ppermute(held, "dp", [(i, i ^ 1) for i in range(lines)])

    line = lax.axis_index("dp")
    z, core = line // 2, line % 2
    sign = 1 - 2 * core
    index = jnp.arange(chips, dtype=jnp.int32)
    ahead = jnp.zeros_like(index)
    reach, bit = chips // 2, 0
    while reach >= 1:
        ahead += ((index >> bit) & 1) * reach
        reach, bit = reach // 2, bit + 1
    place = jnp.concatenate(
        [
            ((z + sign * ahead) % chips) * 2 + core,
            ((z - sign * ahead) % chips) * 2 + (1 - core),
        ]
    ).astype(jnp.int32)

    pair_index = jnp.arange(HALF, dtype=F32)
    frequency = jnp.power(F32(10000.0), -2.0 * pair_index / ROPE)
    positions = (lengths[:, None] + jnp.arange(steps, dtype=jnp.int32)[None, :]).astype(F32)
    angles = positions[..., None] * frequency
    cosine = jnp.cos(angles)
    sine = jnp.sin(angles)
    cos = jnp.concatenate([cosine, cosine], axis=-1)
    sin = jnp.concatenate([-sine, sine], axis=-1)
    cos_pair = jnp.concatenate([cos, cos], axis=-1).reshape(rows * steps, 2 * ROPE)
    sin_pair = jnp.concatenate([sin, sin], axis=-1).reshape(rows * steps, 2 * ROPE)
    cos = cos.reshape(rows, steps * ROPE)
    sin = sin.reshape(rows, steps * ROPE)

    fresh, fresh_lse = fresh_part(queries, new_latent, cos_pair, sin_pair)
    live = jnp.clip(lengths - lax.axis_index("ctx") * span, 0, span)
    partial = attend(live, gathered, cos, sin, latent_cache)
    got = lax.all_to_all(partial, "ctx", 0, 0, tiled=True)
    return merge(place, got, fresh, fresh_lse, held, other, steps, rows)


def solution(mesh):
    placed = (
        P(None, "dp", "ctx", None),
        P("dp", "ctx", None),
        P(None, "dp", None),
        P("dp"),
        P("ctx", "dp", None),
    )
    return jax.shard_map(
        body, mesh=mesh, in_specs=placed, out_specs=P(None, "dp", "ctx", None), check_vma=False
    )
```

```python
import functools

import jax
import jax.numpy as jnp
from jax import lax
from jax.experimental import pallas as pl
from jax.experimental.pallas import tpu as pltpu
from jax.sharding import PartitionSpec as P

LAT = 512
ROPE = 64
HALF = 32
NOPE = 128
SCALE = (NOPE + ROPE) ** (-0.5)
LOG2E = 1.4426950408889634
FLOOR = -1e30
F32 = jnp.float32
BF16 = jnp.bfloat16
NT = (((1,), (1,)), ((), ()))


def vmem():
    return pl.BlockSpec(memory_space=pltpu.VMEM)


def smem():
    return pl.BlockSpec(memory_space=pltpu.SMEM)


def swap_halves(x):
    lane = lax.broadcasted_iota(jnp.int32, x.shape, x.ndim - 1)
    width = x.shape[-1]
    ahead = pltpu.roll(x, width - HALF, x.ndim - 1)
    behind = pltpu.roll(x, HALF, x.ndim - 1)
    return jnp.where(lane % ROPE < HALF, ahead, behind)


def pack_kernel(q_ref, out_ref):
    steps, rows, heads, _ = q_ref.shape
    parts = []
    rotary = []
    for r in range(rows):
        for s in range(steps):
            block = q_ref[s, r].astype(F32)
            parts.append(block[:, :LAT])
            rotary.append(block[:, LAT:])
    parts.append(jnp.concatenate(rotary, axis=1))
    whole = jnp.concatenate(parts, axis=0).astype(BF16)
    for d in range(out_ref.shape[0]):
        out_ref[d] = whole


def pack_queries(queries, shards):
    steps, rows, heads, _ = queries.shape
    count = steps * rows * heads
    return pl.pallas_call(
        pack_kernel,
        out_shape=jax.ShapeDtypeStruct((shards, count + heads, LAT), BF16),
        in_specs=[vmem()],
        out_specs=vmem(),
        name="pack_queries",
    )(queries)


def fresh_kernel(
    q_ref, new_ref, cos_ref, sin_ref, up_ref, mixed_ref, lse_ref, wide_cos_ref, wide_sin_ref, near_ref
):
    steps, rows, heads, _ = q_ref.shape
    count = rows * steps * heads
    keys = rows * steps
    near_ref[...] = up_ref[...]
    q_lat = []
    q_rot = []
    key_lat = []
    key_rot = []
    for r in range(rows):
        for s in range(steps):
            cos = cos_ref[r, s : s + 1]
            sin = sin_ref[r, s : s + 1]
            row_cos = jnp.concatenate([cos, cos, cos, cos], axis=1)
            row_sin = jnp.concatenate([-sin, sin, -sin, sin], axis=1)
            wide_cos_ref[r : r + 1, s * ROPE : (s + 1) * ROPE] = row_cos[:, :ROPE]
            wide_sin_ref[r : r + 1, s * ROPE : (s + 1) * ROPE] = row_sin[:, :ROPE]
            block = q_ref[s, r].astype(F32)
            q_lat.append(block[:, :LAT])
            wide = jnp.concatenate([block[:, LAT:], block[:, LAT:]], axis=1)
            q_rot.append(wide * row_cos + swap_halves(wide) * row_sin)
            key = new_ref[s, r : r + 1].astype(F32)
            key_lat.append(key[:, :LAT])
            wide = jnp.concatenate([key[:, LAT:], key[:, LAT:]], axis=1)
            wide = jnp.broadcast_to(wide, (8, 2 * ROPE))
            wide = wide * row_cos + swap_halves(wide) * row_sin
            key_rot.append(wide[:1])
    q_lat = jnp.concatenate(q_lat, axis=0).astype(BF16)
    q_rot = jnp.concatenate(q_rot, axis=0)[:, :ROPE].astype(BF16)
    pad = jnp.zeros((128 - keys, LAT), F32)
    key_lat = jnp.concatenate(key_lat + [pad], axis=0).astype(BF16)
    key_rot = jnp.concatenate(key_rot + [pad[:, : 2 * ROPE]], axis=0)[:, :ROPE].astype(BF16)
    scores = lax.dot_general(q_lat, key_lat, NT, preferred_element_type=F32)
    scores += lax.dot_general(q_rot, key_rot, NT, preferred_element_type=F32)
    scores *= SCALE
    query = lax.broadcasted_iota(jnp.int32, (count, 128), 0) // heads
    key = lax.broadcasted_iota(jnp.int32, (count, 128), 1)
    valid = (key <= query) & (key // steps == query // steps)
    scores = jnp.where(valid, scores, FLOOR)
    top = jnp.max(scores, axis=1, keepdims=True)
    weights = jnp.where(valid, jnp.exp(scores - top), 0.0)
    total = jnp.sum(weights, axis=1, keepdims=True)
    mixed = jnp.dot(weights.astype(BF16), key_lat, preferred_element_type=F32)
    mixed_ref[...] = mixed / total
    lse_ref[...] = as_rows((top + jnp.log(total)).reshape(rows, steps * heads, 1))


def as_rows(column):
    n, span, _ = column.shape
    row = lax.broadcasted_iota(jnp.int32, (n, span, 128), 1)
    lane = lax.broadcasted_iota(jnp.int32, (n, span, 128), 2)
    return jnp.sum(jnp.where(row == lane, column, 0.0), axis=1)


def fresh_part(queries, new_latent, cos, sin, value_up):
    steps, rows, heads, _ = queries.shape
    count = steps * rows * heads
    return pl.pallas_call(
        fresh_kernel,
        out_shape=(
            jax.ShapeDtypeStruct((count, LAT), F32),
            jax.ShapeDtypeStruct((rows, 128), F32),
            jax.ShapeDtypeStruct((rows, steps * ROPE), F32),
            jax.ShapeDtypeStruct((rows, steps * ROPE), F32),
            jax.ShapeDtypeStruct(value_up.shape, BF16),
        ),
        in_specs=[vmem()] * 5,
        out_specs=(vmem(),) * 5,
        cost_estimate=pl.CostEstimate(flops=10**11, bytes_accessed=0, transcendentals=0),
        name="fresh_part",
    )(queries, new_latent, cos, sin, value_up)


def attend_kernel(lengths_ref, q_ref, cos_ref, sin_ref, cache_ref, out_ref, keys_ref, q_scr, sems):
    rows, _, span = cache_ref.shape
    shards, stride, _ = q_ref.shape
    heads = 8
    count = stride - heads
    copies = [
        pltpu.make_async_copy(cache_ref.at[r], keys_ref.at[r], sems.at[r]) for r in range(rows)
    ]
    for copy in copies:
        copy.start()
    per_row = count // rows
    steps = per_row // heads
    packed = q_ref[:, count:, :].astype(F32).reshape(shards * heads, LAT)
    first_slot = lax.axis_index("ctx") * span
    scored = []
    for r in range(rows):
        live = lengths_ref[r] - first_slot
        q_scr[r, :, :LAT] = q_ref[:, r * per_row : (r + 1) * per_row, :].reshape(
            shards * per_row, LAT
        )
        width = steps * ROPE
        part = packed[:, r * width : (r + 1) * width]
        turned = part * cos_ref[r : r + 1] + swap_halves(part) * sin_ref[r : r + 1]
        turned = jnp.stack(
            [
                turned[:, s * ROPE : (s + 1) * ROPE].reshape(shards, heads, ROPE)
                for s in range(steps)
            ],
            axis=1,
        ).reshape(shards * per_row, ROPE)
        q_scr[r, :, LAT:] = turned.astype(BF16)
        copies[r].wait()
        scores = jnp.dot(q_scr[r], keys_ref[r], preferred_element_type=F32)
        slot = lax.broadcasted_iota(jnp.int32, scores.shape, 1)
        scored.append(jnp.where(slot < live, scores, FLOOR))
    lse_rows = []
    for r in range(rows):
        scores = scored[r]
        top = jnp.max(scores, axis=1, keepdims=True)
        weights = jnp.exp2((scores - top) * (SCALE * LOG2E))
        total = jnp.sum(weights, axis=1, keepdims=True)
        mixed = lax.dot_general(
            weights.astype(BF16), keys_ref[r, :LAT, :], NT, preferred_element_type=F32
        )
        mixed = (mixed * (1.0 / total)).astype(BF16).reshape(shards, per_row, LAT)
        for lanes in range(LAT // 128):
            first = lanes * count + r * per_row
            out_ref[:, first : first + per_row, :] = mixed[:, :, lanes * 128 : (lanes + 1) * 128]
        lse = jnp.where(lengths_ref[r] > first_slot, top * SCALE + jnp.log(total), FLOOR)
        lse_rows.append(as_rows(lse.reshape(shards, per_row, 1)))
    tail = jnp.zeros((shards, heads, 128), F32)
    which = lax.broadcasted_iota(jnp.int32, tail.shape, 1)
    for r in range(rows):
        rest = lse_rows[r]
        for term in range(3):
            piece = rest.astype(BF16).astype(F32)
            tail = jnp.where(which == 3 * r + term, piece[:, None, :], tail)
            rest = rest - piece
    out_ref[:, LAT // 128 * count :, :] = tail.astype(BF16)


def attend(lengths, gathered, cos, sin, keys):
    rows, width, span = keys.shape
    shards, stride, _ = gathered.shape
    per_row = (stride - 8) // rows
    return pl.pallas_call(
        attend_kernel,
        out_shape=jax.ShapeDtypeStruct((shards, (stride - 8) * LAT // 128 + 8, 128), BF16),
        in_specs=[smem()] + [vmem()] * 3 + [pl.BlockSpec(memory_space=pltpu.HBM)],
        out_specs=vmem(),
        scratch_shapes=[
            pltpu.VMEM(keys.shape, BF16),
            pltpu.VMEM((rows, shards * per_row, width), BF16),
            pltpu.SemaphoreType.DMA((rows,)),
        ],
        compiler_params=pltpu.CompilerParams(vmem_limit_bytes=50 * 1024 * 1024),
        cost_estimate=pl.CostEstimate(
            flops=2 * rows * shards * per_row * span * (width + LAT),
            bytes_accessed=keys.size * 2 + gathered.size * 4,
            transcendentals=rows * shards * per_row * span,
        ),
        name="attend",
    )(lengths, gathered, cos, sin, keys)


def merge_kernel(offsets, got_ref, fresh_ref, fresh_lse_ref, *refs):
    *up_refs, out_ref, up = refs
    steps, rows, heads, _ = out_ref.shape
    shards = got_ref.shape[0]
    count = steps * rows * heads
    per_row = count // rows
    line = lax.axis_index("dp")
    chips = lax.axis_size("dp") // 2
    z = line // 2
    own = 1 - 2 * (line % 2)
    for ref, mine, spans in zip(up_refs, (1, 1, 1, -1, -1), offsets):
        depth = ref.shape[2]
        for b, offset in enumerate(spans):
            chip = (z + own * (mine * offset) + chips) % chips
            up[:, pl.ds(pl.multiple_of(chip * depth, depth), depth), :] = ref[b]
    tail = got_ref[:, LAT // 128 * count :, :].astype(F32)
    sub = lax.broadcasted_iota(jnp.int32, (per_row, 128), 0)
    lane = lax.broadcasted_iota(jnp.int32, (per_row, 128), 1)
    eye = sub == lane

    def column(row):
        return jnp.sum(jnp.where(eye, row, 0.0), axis=1, keepdims=True)

    merged = []
    for r in range(rows):
        spread = tail[:, 3 * r] + tail[:, 3 * r + 1] + tail[:, 3 * r + 2]
        own = fresh_lse_ref[r : r + 1]
        top = jnp.maximum(jnp.max(spread, axis=0, keepdims=True), own)
        factor = jnp.exp(spread - top)
        own_factor = jnp.exp(own - top)
        scale = 1.0 / (jnp.sum(factor, axis=0, keepdims=True) + own_factor)
        factor = factor * scale
        first = r * per_row
        total = column(own_factor * scale) * fresh_ref[first : first + per_row]
        for d in range(shards):
            piece = jnp.concatenate(
                [
                    got_ref[d, lanes * count + first : lanes * count + first + per_row, :]
                    for lanes in range(LAT // 128)
                ],
                axis=1,
            ).astype(F32)
            total += column(factor[d : d + 1]) * piece
        merged.append(total)
    latent = jnp.concatenate(merged, axis=0).astype(BF16)
    head = lax.broadcasted_iota(jnp.int32, (count, 128), 0) % heads
    result = jnp.zeros((count, 128), F32)
    for h in range(heads):
        product = jnp.dot(latent, up[h], preferred_element_type=F32)
        result = jnp.where(head == h, product, result)
    for r in range(rows):
        for s in range(steps):
            first = (r * steps + s) * heads
            out_ref[s, r] = result[first : first + heads]


def merge(got, fresh, fresh_lse, ups, offsets, steps, rows):
    _, heads, depth, width = ups[0].shape
    return pl.pallas_call(
        functools.partial(merge_kernel, offsets),
        out_shape=jax.ShapeDtypeStruct((steps, rows, heads, width), F32),
        in_specs=[vmem()] * (3 + len(ups)),
        out_specs=vmem(),
        scratch_shapes=[pltpu.VMEM((heads, LAT, width), BF16)],
        compiler_params=pltpu.CompilerParams(vmem_limit_bytes=16 * 1024 * 1024),
        name="merge",
    )(got, fresh, fresh_lse, *ups)


def body(queries, latent_cache, new_latent, lengths, value_up):
    steps, rows, heads, _ = queries.shape
    shards = lax.axis_size("ctx")
    lines = lax.axis_size("dp")
    chips = lines // 2

    def from_line(x, reach):
        pairs = []
        for line in range(lines):
            z, core = line // 2, line % 2
            sign = 1 - 2 * core
            pairs.append((((z + sign * reach) % chips) * 2 + core, line))
        return lax.ppermute(x, "dp", pairs)

    def from_core(x):
        return lax.ppermute(x, "dp", [(i, i ^ 1) for i in range(lines)])

    pair_index = jnp.arange(HALF, dtype=F32)
    frequency = jnp.power(F32(10000.0), -2.0 * pair_index / ROPE)
    positions = (lengths[:, None] + jnp.arange(steps, dtype=jnp.int32)[None, :]).astype(F32)
    angles = positions[..., None] * frequency
    packed = pack_queries(queries, shards)
    packed, value_up = lax.optimization_barrier((packed, value_up))
    gathered = lax.all_to_all(packed, "ctx", 0, 0, tiled=True)

    fresh, fresh_lse, cos, sin, near = fresh_part(
        queries, new_latent, jnp.cos(angles), jnp.sin(angles), value_up
    )
    near = lax.all_gather(
        near, "dp", axis=1, tiled=True, axis_index_groups=[[2 * z, 2 * z + 1] for z in range(chips)]
    )[None]
    held = jnp.concatenate([near, from_line(near, 4)], axis=0)
    second = from_line(held, 2)
    partial = attend(lengths, gathered, cos, sin, jnp.swapaxes(latent_cache, 1, 2))
    partial, second = lax.optimization_barrier((partial, second))
    got = lax.all_to_all(partial, "ctx", 0, 0, tiled=True)
    held = jnp.concatenate([held, second], axis=0)
    third = from_line(held, 1)
    eighth = from_line(third[-1:], 1)
    ups = (held, third, eighth, from_core(held), from_core(third))
    even, odd = (0, 4, 2, 6), (1, 5, 3, 7)
    return merge(got, fresh, fresh_lse, ups, (even, odd, (8,), even, odd), steps, rows)


def solution(mesh):
    placed = (
        P(None, "dp", "ctx", None),
        P("dp", "ctx", None),
        P(None, "dp", None),
        P("dp"),
        P("ctx", "dp", None),
    )
    return jax.shard_map(
        body, mesh=mesh, in_specs=placed, out_specs=P(None, "dp", "ctx", None), check_vma=False
    )
```

```python
import functools

import jax
import jax.numpy as jnp
import numpy as np
from jax import lax
from jax.experimental import pallas as pl
from jax.experimental.pallas import tpu as pltpu
from jax.sharding import PartitionSpec as P

LAT = 512
ROPE = 64
HALF = 32
NOPE = 128
SCALE = (NOPE + ROPE) ** (-0.5)
LOG2E = 1.4426950408889634
FLOOR = -1e30
F32 = jnp.float32
BF16 = jnp.bfloat16
NT = (((1,), (1,)), ((), ()))


def vmem():
    return pl.BlockSpec(memory_space=pltpu.VMEM)


def smem():
    return pl.BlockSpec(memory_space=pltpu.SMEM)


def swap_halves(x):
    lane = lax.broadcasted_iota(jnp.int32, x.shape, x.ndim - 1)
    width = x.shape[-1]
    ahead = pltpu.roll(x, width - HALF, x.ndim - 1)
    behind = pltpu.roll(x, HALF, x.ndim - 1)
    return jnp.where(lane % ROPE < HALF, ahead, behind)


def pack_kernel(q_ref, out_ref):
    steps, rows, heads, _ = q_ref.shape
    parts = []
    rotary = []
    for r in range(rows):
        for s in range(steps):
            block = q_ref[s, r].astype(F32)
            parts.append(block[:, :LAT])
            rotary.append(block[:, LAT:])
    parts.append(jnp.concatenate(rotary, axis=1))
    whole = jnp.concatenate(parts, axis=0).astype(BF16)
    for d in range(out_ref.shape[0]):
        out_ref[d] = whole


def pack_queries(queries, shards):
    steps, rows, heads, _ = queries.shape
    count = steps * rows * heads
    return pl.pallas_call(
        pack_kernel,
        out_shape=jax.ShapeDtypeStruct((shards, count + heads, LAT), BF16),
        in_specs=[vmem()],
        out_specs=vmem(),
        name="pack_queries",
    )(queries)


def rotation(lengths_ref, steps, shape, step_of, row_of):
    row = lax.broadcasted_iota(jnp.int32, shape, 0)
    lane = lax.broadcasted_iota(jnp.int32, shape, 1)
    which = row_of(row)
    position = jnp.zeros(shape, jnp.int32)
    for r in range(lengths_ref.shape[0]):
        position = jnp.where(which == r, lengths_ref[r], position)
    position += step_of(row, lane)
    frequency = jnp.zeros(shape, F32)
    for i in range(HALF):
        value = float(np.float32(10000.0 ** (-2.0 * i / ROPE)))
        frequency = jnp.where(lane % HALF == i, value, frequency)
    angle = position.astype(F32) * frequency
    sine = jnp.sin(angle)
    return jnp.cos(angle), jnp.where(lane % ROPE < HALF, -sine, sine)


def fresh_kernel(lengths_ref, q_ref, new_ref, mixed_ref, lse_ref):
    steps, rows, heads, _ = q_ref.shape
    count = rows * steps * heads
    keys = rows * steps
    cos, sin = rotation(
        lengths_ref, steps, (keys, 2 * ROPE), lambda row, _: row % steps, lambda row: row // steps
    )
    q_lat = []
    q_rot = []
    key_lat = []
    key_rot = []
    for r in range(rows):
        for s in range(steps):
            row_cos = cos[r * steps + s : r * steps + s + 1]
            row_sin = sin[r * steps + s : r * steps + s + 1]
            block = q_ref[s, r].astype(F32)
            q_lat.append(block[:, :LAT])
            wide = jnp.concatenate([block[:, LAT:], block[:, LAT:]], axis=1)
            q_rot.append(wide * row_cos + swap_halves(wide) * row_sin)
            key = new_ref[s, r : r + 1].astype(F32)
            key_lat.append(key[:, :LAT])
            wide = jnp.concatenate([key[:, LAT:], key[:, LAT:]], axis=1)
            wide = jnp.broadcast_to(wide, (8, 2 * ROPE))
            wide = wide * row_cos + swap_halves(wide) * row_sin
            key_rot.append(wide[:1])
    q_lat = jnp.concatenate(q_lat, axis=0).astype(BF16)
    q_rot = jnp.concatenate(q_rot, axis=0)[:, :ROPE].astype(BF16)
    pad = jnp.zeros((128 - keys, LAT), F32)
    key_lat = jnp.concatenate(key_lat + [pad], axis=0).astype(BF16)
    key_rot = jnp.concatenate(key_rot + [pad[:, : 2 * ROPE]], axis=0)[:, :ROPE].astype(BF16)
    scores = lax.dot_general(q_lat, key_lat, NT, preferred_element_type=F32)
    scores += lax.dot_general(q_rot, key_rot, NT, preferred_element_type=F32)
    scores *= SCALE
    query = lax.broadcasted_iota(jnp.int32, (count, 128), 0) // heads
    key = lax.broadcasted_iota(jnp.int32, (count, 128), 1)
    valid = (key <= query) & (key // steps == query // steps)
    scores = jnp.where(valid, scores, FLOOR)
    top = jnp.max(scores, axis=1, keepdims=True)
    weights = jnp.where(valid, jnp.exp(scores - top), 0.0)
    total = jnp.sum(weights, axis=1, keepdims=True)
    mixed = jnp.dot(weights.astype(BF16), key_lat, preferred_element_type=F32)
    mixed_ref[...] = mixed / total
    lse_ref[...] = as_rows((top + jnp.log(total)).reshape(rows, steps * heads, 1))


def as_rows(column):
    n, span, _ = column.shape
    row = lax.broadcasted_iota(jnp.int32, (n, span, 128), 1)
    lane = lax.broadcasted_iota(jnp.int32, (n, span, 128), 2)
    return jnp.sum(jnp.where(row == lane, column, 0.0), axis=1)


def fresh_part(lengths, queries, new_latent):
    steps, rows, heads, _ = queries.shape
    count = steps * rows * heads
    return pl.pallas_call(
        fresh_kernel,
        out_shape=(
            jax.ShapeDtypeStruct((count, LAT), F32),
            jax.ShapeDtypeStruct((rows, 128), F32),
        ),
        in_specs=[smem()] + [vmem()] * 2,
        out_specs=(vmem(),) * 2,
        name="fresh_part",
    )(lengths, queries, new_latent)


CHUNK = 512
PARTS = 2


def attend_kernel(lengths_ref, q_ref, cache_ref, out_hbm, *scratch):
    keys_ref, q_scr, s_scr, p_scr, out_ref, sems, out_sems = scratch
    rows, width, span = cache_ref.shape
    shards, stride, _ = q_ref.shape
    heads = 8
    count = stride - heads
    per_row = count // rows
    steps = per_row // heads
    many = shards * per_row
    deep = width // PARTS
    copies = [
        [
            pltpu.make_async_copy(
                cache_ref.at[r, pl.ds(part * deep, deep)],
                keys_ref.at[r, pl.ds(part * deep, deep)],
                sems.at[r, part],
            )
            for part in range(PARTS)
        ]
        for r in range(rows)
    ]
    for copy in copies[0]:
        copy.start()
    packed = q_ref[:, count:, :].astype(F32).reshape(shards * heads, LAT)
    first_slot = lax.axis_index("ctx") * span
    pad = keys_ref.shape[1] - width
    cos, sin = rotation(
        lengths_ref, steps, (8, steps * ROPE), lambda _, lane: lane // ROPE, lambda row: row
    )
    for r in range(rows):
        live = lengths_ref[r] - first_slot
        slot = lax.broadcasted_iota(jnp.int32, (pad, span), 1)
        line = lax.broadcasted_iota(jnp.int32, (pad, span), 0)
        keys_ref[r, width:, :] = jnp.where((line == 0) & (slot >= live), FLOOR, 0.0).astype(BF16)
        q_scr[r, :, :LAT] = q_ref[:, r * per_row : (r + 1) * per_row, :].reshape(many, LAT)
        part = packed[:, r * steps * ROPE : (r + 1) * steps * ROPE]
        turned = part * cos[r : r + 1] + swap_halves(part) * sin[r : r + 1]
        turned = jnp.stack(
            [
                turned[:, s * ROPE : (s + 1) * ROPE].reshape(shards, heads, ROPE)
                for s in range(steps)
            ],
            axis=1,
        ).reshape(many, ROPE)
        lane = lax.broadcasted_iota(jnp.int32, (many, pad), 1)
        one = jnp.where(lane == 0, 1.0, 0.0)
        q_scr[r, :, LAT:] = jnp.concatenate([turned, one], axis=1).astype(BF16)

    half = LAT // 128 * per_row
    outs = [
        pltpu.make_async_copy(out_ref.at[:, pl.ds(0, half)], out_hbm.at[:, pl.ds(0, half)], out_sems.at[0]),
        pltpu.make_async_copy(
            out_ref.at[:, pl.ds(half, out_hbm.shape[1] - half)],
            out_hbm.at[:, pl.ds(half, out_hbm.shape[1] - half)],
            out_sems.at[1],
        ),
    ]

    def score(r, first, top):
        part = jnp.dot(
            q_scr[r], keys_ref[r, :, first : first + CHUNK], preferred_element_type=F32
        )
        s_scr[r, :, first : first + CHUNK] = part
        for lanes in range(0, CHUNK, 128):
            block = part[:, lanes : lanes + 128]
            top = block if top is None else jnp.maximum(top, block)
        return top

    def weigh(r, first, level, total):
        part = jnp.exp2((s_scr[r, :, first : first + CHUNK] - level) * (SCALE * LOG2E))
        p_scr[r, :, first : first + CHUNK] = part.astype(BF16)
        for lanes in range(0, CHUNK, 128):
            block = part[:, lanes : lanes + 128]
            total = block if total is None else total + block
        return total

    def mix(r):
        return lax.dot_general(p_scr[r], keys_ref[r, :LAT, :], NT, preferred_element_type=F32)

    def finish(r, level, total, mixed):
        total = jnp.sum(total, axis=1, keepdims=True)
        mixed = (mixed * (1.0 / total)).astype(BF16).reshape(shards, per_row, LAT)
        for lanes in range(LAT // 128):
            first = (r * (LAT // 128) + lanes) * per_row
            out_ref[:, first : first + per_row, :] = mixed[:, :, lanes * 128 : (lanes + 1) * 128]
        if r == 0:
            outs[0].start()
        lse = jnp.where(lengths_ref[r] > first_slot, level * SCALE + jnp.log(total), FLOOR)
        return as_rows(lse.reshape(shards, per_row, 1))

    levels = []
    totals = [None] * rows
    for r in range(rows):
        for copy in copies[r]:
            copy.wait()
        if r + 1 < rows:
            for copy in copies[r + 1]:
                copy.start()
        top = None
        for first in range(0, span, CHUNK):
            top = score(r, first, top)
        levels.append(jnp.max(top, axis=1, keepdims=True))
        if r == 0:
            for first in range(0, span, CHUNK):
                totals[0] = weigh(0, first, levels[0], totals[0])
    lse_rows = []
    for r in range(rows):
        mixed = mix(r)
        if r == rows - 2:
            for first in range(0, span, CHUNK):
                totals[r + 1] = weigh(r + 1, first, levels[r + 1], totals[r + 1])
        lse_rows.append(finish(r, levels[r], totals[r], mixed))
    tail = jnp.zeros((shards, heads, 128), F32)
    which = lax.broadcasted_iota(jnp.int32, tail.shape, 1)
    for r in range(rows):
        rest = lse_rows[r]
        for term in range(3):
            piece = rest.astype(BF16).astype(F32)
            tail = jnp.where(which == 3 * r + term, piece[:, None, :], tail)
            rest = rest - piece
    out_ref[:, LAT // 128 * count :, :] = tail.astype(BF16)
    outs[1].start()
    for out in outs:
        out.wait()


def attend(lengths, gathered, keys):
    rows, width, span = keys.shape
    shards, stride, _ = gathered.shape
    many = (stride - 8) // rows * shards
    padded = width + 64
    return pl.pallas_call(
        attend_kernel,
        out_shape=jax.ShapeDtypeStruct((shards, (stride - 8) * LAT // 128 + 8, 128), BF16),
        in_specs=[smem(), vmem(), pl.BlockSpec(memory_space=pltpu.HBM)],
        out_specs=pl.BlockSpec(memory_space=pltpu.HBM),
        scratch_shapes=[
            pltpu.VMEM((rows, padded, span), BF16),
            pltpu.VMEM((rows, many, padded), BF16),
            pltpu.VMEM((rows, many, span), F32),
            pltpu.VMEM((rows, many, span), BF16),
            pltpu.VMEM((shards, (stride - 8) * LAT // 128 + 8, 128), BF16),
            pltpu.SemaphoreType.DMA((rows, PARTS)),
            pltpu.SemaphoreType.DMA((2,)),
        ],
        compiler_params=pltpu.CompilerParams(vmem_limit_bytes=50 * 1024 * 1024),
        cost_estimate=pl.CostEstimate(
            flops=2 * rows * many * span * (width + LAT),
            bytes_accessed=keys.size * 2 + gathered.size * 4,
            transcendentals=rows * many * span,
        ),
        name="attend",
    )(lengths, gathered, keys)


def merge_kernel(offsets, got_ref, fresh_ref, fresh_lse_ref, *refs):
    *up_refs, out_ref, up = refs
    steps, rows, heads, _ = out_ref.shape
    shards = got_ref.shape[0]
    count = steps * rows * heads
    per_row = count // rows
    line = lax.axis_index("dp")
    chips = lax.axis_size("dp") // 2
    z = line // 2
    own = 1 - 2 * (line % 2)
    for ref, mine, spans in zip(up_refs, (1, 1, 1, -1, -1), offsets):
        depth = ref.shape[2]
        for b, offset in enumerate(spans):
            chip = (z + own * (mine * offset) + chips) % chips
            up[:, pl.ds(pl.multiple_of(chip * depth, depth), depth), :] = ref[b]
    tail = got_ref[:, LAT // 128 * count :, :].astype(F32)
    sub = lax.broadcasted_iota(jnp.int32, (per_row, 128), 0)
    lane = lax.broadcasted_iota(jnp.int32, (per_row, 128), 1)
    eye = sub == lane

    def column(row):
        return jnp.sum(jnp.where(eye, row, 0.0), axis=1, keepdims=True)

    merged = []
    for r in range(rows):
        spread = tail[:, 3 * r] + tail[:, 3 * r + 1] + tail[:, 3 * r + 2]
        own = fresh_lse_ref[r : r + 1]
        top = jnp.maximum(jnp.max(spread, axis=0, keepdims=True), own)
        factor = jnp.exp(spread - top)
        own_factor = jnp.exp(own - top)
        scale = 1.0 / (jnp.sum(factor, axis=0, keepdims=True) + own_factor)
        factor = factor * scale
        first = r * per_row
        total = column(own_factor * scale) * fresh_ref[first : first + per_row]
        for d in range(shards):
            piece = jnp.concatenate(
                [
                    got_ref[d, lanes * per_row : (lanes + 1) * per_row, :]
                    for lanes in range(r * (LAT // 128), (r + 1) * (LAT // 128))
                ],
                axis=1,
            ).astype(F32)
            total += column(factor[d : d + 1]) * piece
        merged.append(total)
    latent = jnp.concatenate(merged, axis=0).astype(BF16)
    head = lax.broadcasted_iota(jnp.int32, (count, 128), 0) % heads
    result = jnp.zeros((count, 128), F32)
    for h in range(heads):
        product = jnp.dot(latent, up[h], preferred_element_type=F32)
        result = jnp.where(head == h, product, result)
    for r in range(rows):
        for s in range(steps):
            first = (r * steps + s) * heads
            out_ref[s, r] = result[first : first + heads]


def merge(got, fresh, fresh_lse, ups, offsets, steps, rows):
    _, heads, depth, width = ups[0].shape
    return pl.pallas_call(
        functools.partial(merge_kernel, offsets),
        out_shape=jax.ShapeDtypeStruct((steps, rows, heads, width), F32),
        in_specs=[vmem()] * (3 + len(ups)),
        out_specs=vmem(),
        scratch_shapes=[pltpu.VMEM((heads, LAT, width), BF16)],
        compiler_params=pltpu.CompilerParams(vmem_limit_bytes=16 * 1024 * 1024),
        name="merge",
    )(got, fresh, fresh_lse, *ups)


def body(queries, latent_cache, new_latent, lengths, value_up):
    steps, rows, heads, _ = queries.shape
    shards = lax.axis_size("ctx")
    lines = lax.axis_size("dp")
    chips = lines // 2

    def from_line(x, reach):
        pairs = []
        for line in range(lines):
            z, core = line // 2, line % 2
            sign = 1 - 2 * core
            pairs.append((((z + sign * reach) % chips) * 2 + core, line))
        return lax.ppermute(x, "dp", pairs)

    def from_core(x):
        return lax.ppermute(x, "dp", [(i, i ^ 1) for i in range(lines)])

    packed = pack_queries(queries, shards)
    packed, value_up, lengths = lax.optimization_barrier((packed, value_up, lengths))
    gathered = lax.all_to_all(packed, "ctx", 0, 0, tiled=True)

    near = lax.all_gather(
        value_up, "dp", axis=1, tiled=True,
        axis_index_groups=[[2 * z, 2 * z + 1] for z in range(chips)],
    )[None]
    first = from_line(near, 4)

    fresh, fresh_lse = fresh_part(lengths, queries, new_latent)
    held = jnp.concatenate([near, first], axis=0)
    held, fresh, fresh_lse = lax.optimization_barrier((held, fresh, fresh_lse))
    second = from_line(held, 2)
    partial = attend(lengths, gathered, jnp.swapaxes(latent_cache, 1, 2))
    partial, second = lax.optimization_barrier((partial, second))
    got = lax.all_to_all(partial, "ctx", 0, 0, tiled=True)
    held = jnp.concatenate([held, second], axis=0)
    third = from_line(held, 1)
    eighth = from_line(second[-1:], 2)
    third, eighth = lax.optimization_barrier((third, eighth))
    ups = (held, third, eighth, from_core(held), from_core(third))
    even, odd = (0, 4, 2, 6), (1, 5, 3, 7)
    return merge(got, fresh, fresh_lse, ups, (even, odd, (8,), even, odd), steps, rows)


def solution(mesh):
    placed = (
        P(None, "dp", "ctx", None),
        P("dp", "ctx", None),
        P(None, "dp", None),
        P("dp"),
        P("ctx", "dp", None),
    )
    return jax.shard_map(
        body, mesh=mesh, in_specs=placed, out_specs=P(None, "dp", "ctx", None), check_vma=False
    )
```

```python
import functools

import jax
import jax.numpy as jnp
import numpy as np
from jax import lax
from jax.experimental import pallas as pl
from jax.experimental.pallas import tpu as pltpu
from jax.sharding import PartitionSpec as P

LAT = 512
ROPE = 64
HALF = 32
NOPE = 128
SCALE = (NOPE + ROPE) ** (-0.5)
LOG2E = 1.4426950408889634
FLOOR = -1e30
F32 = jnp.float32
BF16 = jnp.bfloat16
NT = (((1,), (1,)), ((), ()))


def vmem():
    return pl.BlockSpec(memory_space=pltpu.VMEM)


def smem():
    return pl.BlockSpec(memory_space=pltpu.SMEM)


def swap_halves(x):
    lane = lax.broadcasted_iota(jnp.int32, x.shape, x.ndim - 1)
    width = x.shape[-1]
    ahead = pltpu.roll(x, width - HALF, x.ndim - 1)
    behind = pltpu.roll(x, HALF, x.ndim - 1)
    return jnp.where(lane % ROPE < HALF, ahead, behind)


def pack_kernel(q_ref, out_ref):
    steps, rows, heads, _ = q_ref.shape
    parts = []
    rotary = []
    for r in range(rows):
        for s in range(steps):
            block = q_ref[s, r].astype(F32)
            parts.append(block[:, :LAT])
            rotary.append(block[:, LAT:])
    parts.append(jnp.concatenate(rotary, axis=1))
    whole = jnp.concatenate(parts, axis=0).astype(BF16)
    for d in range(out_ref.shape[0]):
        out_ref[d] = whole


def pack_queries(queries, shards):
    steps, rows, heads, _ = queries.shape
    count = steps * rows * heads
    return pl.pallas_call(
        pack_kernel,
        out_shape=jax.ShapeDtypeStruct((shards, count + heads, LAT), BF16),
        in_specs=[vmem()],
        out_specs=vmem(),
        name="pack_queries",
    )(queries)


def rotation(lengths_ref, steps, shape, step_of, row_of):
    row = lax.broadcasted_iota(jnp.int32, shape, 0)
    lane = lax.broadcasted_iota(jnp.int32, shape, 1)
    which = row_of(row)
    position = jnp.zeros(shape, jnp.int32)
    for r in range(lengths_ref.shape[0]):
        position = jnp.where(which == r, lengths_ref[r], position)
    position += step_of(row, lane)
    frequency = jnp.zeros(shape, F32)
    for i in range(HALF):
        value = float(np.float32(10000.0 ** (-2.0 * i / ROPE)))
        frequency = jnp.where(lane % HALF == i, value, frequency)
    angle = position.astype(F32) * frequency
    sine = jnp.sin(angle)
    return jnp.cos(angle), jnp.where(lane % ROPE < HALF, -sine, sine)


def fresh_kernel(lengths_ref, q_ref, new_ref, mixed_ref, lse_ref):
    steps, rows, heads, _ = q_ref.shape
    count = rows * steps * heads
    keys = rows * steps
    cos, sin = rotation(
        lengths_ref, steps, (keys, 2 * ROPE), lambda row, _: row % steps, lambda row: row // steps
    )
    q_lat = []
    q_rot = []
    key_lat = []
    key_rot = []
    for r in range(rows):
        for s in range(steps):
            row_cos = cos[r * steps + s : r * steps + s + 1]
            row_sin = sin[r * steps + s : r * steps + s + 1]
            block = q_ref[s, r].astype(F32)
            q_lat.append(block[:, :LAT])
            wide = jnp.concatenate([block[:, LAT:], block[:, LAT:]], axis=1)
            q_rot.append(wide * row_cos + swap_halves(wide) * row_sin)
            key = new_ref[s, r : r + 1].astype(F32)
            key_lat.append(key[:, :LAT])
            wide = jnp.concatenate([key[:, LAT:], key[:, LAT:]], axis=1)
            wide = jnp.broadcast_to(wide, (8, 2 * ROPE))
            wide = wide * row_cos + swap_halves(wide) * row_sin
            key_rot.append(wide[:1])
    q_lat = jnp.concatenate(q_lat, axis=0).astype(BF16)
    q_rot = jnp.concatenate(q_rot, axis=0)[:, :ROPE].astype(BF16)
    pad = jnp.zeros((128 - keys, LAT), F32)
    key_lat = jnp.concatenate(key_lat + [pad], axis=0).astype(BF16)
    key_rot = jnp.concatenate(key_rot + [pad[:, : 2 * ROPE]], axis=0)[:, :ROPE].astype(BF16)
    scores = lax.dot_general(q_lat, key_lat, NT, preferred_element_type=F32)
    scores += lax.dot_general(q_rot, key_rot, NT, preferred_element_type=F32)
    scores *= SCALE
    query = lax.broadcasted_iota(jnp.int32, (count, 128), 0) // heads
    key = lax.broadcasted_iota(jnp.int32, (count, 128), 1)
    valid = (key <= query) & (key // steps == query // steps)
    scores = jnp.where(valid, scores, FLOOR)
    top = jnp.max(scores, axis=1, keepdims=True)
    weights = jnp.where(valid, jnp.exp(scores - top), 0.0)
    total = jnp.sum(weights, axis=1, keepdims=True)
    mixed = jnp.dot(weights.astype(BF16), key_lat, preferred_element_type=F32)
    mixed_ref[...] = mixed / total
    lse_ref[...] = as_rows((top + jnp.log(total)).reshape(rows, steps * heads, 1))


def as_rows(column):
    n, span, _ = column.shape
    row = lax.broadcasted_iota(jnp.int32, (n, span, 128), 1)
    lane = lax.broadcasted_iota(jnp.int32, (n, span, 128), 2)
    return jnp.sum(jnp.where(row == lane, column, 0.0), axis=1)


def fresh_part(lengths, queries, new_latent):
    steps, rows, heads, _ = queries.shape
    count = steps * rows * heads
    return pl.pallas_call(
        fresh_kernel,
        out_shape=(
            jax.ShapeDtypeStruct((count, LAT), F32),
            jax.ShapeDtypeStruct((rows, 128), F32),
        ),
        in_specs=[smem()] + [vmem()] * 2,
        out_specs=(vmem(),) * 2,
        name="fresh_part",
    )(lengths, queries, new_latent)


CHUNK = 512
PARTS = 2


def attend_kernel(lengths_ref, q_ref, cache_ref, out_hbm, *scratch):
    keys_ref, q_scr, s_scr, p_scr, out_ref, sems, out_sems = scratch
    rows, width, span = cache_ref.shape
    shards, stride, _ = q_ref.shape
    heads = 8
    count = stride - heads
    per_row = count // rows
    steps = per_row // heads
    many = shards * per_row
    deep = width // PARTS
    copies = [
        [
            pltpu.make_async_copy(
                cache_ref.at[r, pl.ds(part * 256, 256 + 64 * part)],
                keys_ref.at[r, pl.ds(part * 256, 256 + 64 * part)],
                sems.at[r, part],
            )
            for part in range(PARTS)
        ]
        for r in range(rows)
    ]
    for copy in copies[0]:
        copy.start()
    packed = q_ref[:, count:, :].astype(F32).reshape(shards * heads, LAT)
    first_slot = lax.axis_index("ctx") * span
    pad = keys_ref.shape[1] - width
    cos, sin = rotation(
        lengths_ref, steps, (8, steps * ROPE), lambda _, lane: lane // ROPE, lambda row: row
    )
    for r in range(rows):
        live = lengths_ref[r] - first_slot
        slot = lax.broadcasted_iota(jnp.int32, (pad, span), 1)
        line = lax.broadcasted_iota(jnp.int32, (pad, span), 0)
        keys_ref[r, width:, :] = jnp.where((line == 0) & (slot >= live), FLOOR, 0.0).astype(BF16)
        q_scr[r, :, :LAT] = q_ref[:, r * per_row : (r + 1) * per_row, :].reshape(many, LAT)
        part = packed[:, r * steps * ROPE : (r + 1) * steps * ROPE]
        turned = part * cos[r : r + 1] + swap_halves(part) * sin[r : r + 1]
        turned = jnp.stack(
            [
                turned[:, s * ROPE : (s + 1) * ROPE].reshape(shards, heads, ROPE)
                for s in range(steps)
            ],
            axis=1,
        ).reshape(many, ROPE)
        lane = lax.broadcasted_iota(jnp.int32, (many, pad), 1)
        one = jnp.where(lane == 0, 1.0, 0.0)
        q_scr[r, :, LAT:] = jnp.concatenate([turned, one], axis=1).astype(BF16)

    half = LAT // 128 * per_row
    outs = [
        pltpu.make_async_copy(out_ref.at[:, pl.ds(0, half)], out_hbm.at[:, pl.ds(0, half)], out_sems.at[0]),
        pltpu.make_async_copy(
            out_ref.at[:, pl.ds(half, out_hbm.shape[1] - half)],
            out_hbm.at[:, pl.ds(half, out_hbm.shape[1] - half)],
            out_sems.at[1],
        ),
    ]

    def partial_score(r, lo, hi, fresh):
        for first in range(0, span, CHUNK):
            part = jnp.dot(
                q_scr[r, :, lo:hi], keys_ref[r, lo:hi, first : first + CHUNK], preferred_element_type=F32
            )
            if not fresh:
                part += s_scr[r, :, first : first + CHUNK]
            s_scr[r, :, first : first + CHUNK] = part

    def score(r, first, top):
        if r == 0:
            part = s_scr[r, :, first : first + CHUNK]
            part += jnp.dot(q_scr[r, :, 256:], keys_ref[r, 256:, first : first + CHUNK], preferred_element_type=F32)
        else:
            part = jnp.dot(
                q_scr[r], keys_ref[r, :, first : first + CHUNK], preferred_element_type=F32
            )
        s_scr[r, :, first : first + CHUNK] = part
        for lanes in range(0, CHUNK, 128):
            block = part[:, lanes : lanes + 128]
            top = block if top is None else jnp.maximum(top, block)
        return top

    def weigh(r, first, level, total):
        part = jnp.exp2((s_scr[r, :, first : first + CHUNK] - level) * (SCALE * LOG2E))
        p_scr[r, :, first : first + CHUNK] = part.astype(BF16)
        for lanes in range(0, CHUNK, 128):
            block = part[:, lanes : lanes + 128]
            total = block if total is None else total + block
        return total

    def mix(r):
        return lax.dot_general(p_scr[r], keys_ref[r, :LAT, :], NT, preferred_element_type=F32)

    def finish(r, level, total, mixed):
        total = jnp.sum(total, axis=1, keepdims=True)
        mixed = (mixed * (1.0 / total)).astype(BF16).reshape(shards, per_row, LAT)
        for lanes in range(LAT // 128):
            first = (r * (LAT // 128) + lanes) * per_row
            out_ref[:, first : first + per_row, :] = mixed[:, :, lanes * 128 : (lanes + 1) * 128]
        if r == 0:
            outs[0].start()
        lse = jnp.where(lengths_ref[r] > first_slot, level * SCALE + jnp.log(total), FLOOR)
        return as_rows(lse.reshape(shards, per_row, 1))

    levels = []
    totals = [None] * rows
    for r in range(rows):
        copies[r][0].wait()
        if r == 0:
            partial_score(0, 0, 256, True)
        copies[r][1].wait()
        if r + 1 < rows:
            for copy in copies[r + 1]:
                copy.start()
        top = None
        for first in range(0, span, CHUNK):
            top = score(r, first, top)
        levels.append(jnp.max(top, axis=1, keepdims=True))
        if r == 0:
            for first in range(0, span, CHUNK):
                totals[0] = weigh(0, first, levels[0], totals[0])
    lse_rows = []
    for r in range(rows):
        mixed = mix(r)
        if r == rows - 2:
            for first in range(0, span, CHUNK):
                totals[r + 1] = weigh(r + 1, first, levels[r + 1], totals[r + 1])
        lse_rows.append(finish(r, levels[r], totals[r], mixed))
    tail = jnp.zeros((shards, heads, 128), F32)
    which = lax.broadcasted_iota(jnp.int32, tail.shape, 1)
    for r in range(rows):
        rest = lse_rows[r]
        for term in range(3):
            piece = rest.astype(BF16).astype(F32)
            tail = jnp.where(which == 3 * r + term, piece[:, None, :], tail)
            rest = rest - piece
    out_ref[:, LAT // 128 * count :, :] = tail.astype(BF16)
    outs[1].start()
    for out in outs:
        out.wait()


def attend(lengths, gathered, keys):
    rows, width, span = keys.shape
    shards, stride, _ = gathered.shape
    many = (stride - 8) // rows * shards
    padded = width + 64
    return pl.pallas_call(
        attend_kernel,
        out_shape=jax.ShapeDtypeStruct((shards, (stride - 8) * LAT // 128 + 8, 128), BF16),
        in_specs=[smem(), vmem(), pl.BlockSpec(memory_space=pltpu.HBM)],
        out_specs=pl.BlockSpec(memory_space=pltpu.HBM),
        scratch_shapes=[
            pltpu.VMEM((rows, padded, span), BF16),
            pltpu.VMEM((rows, many, padded), BF16),
            pltpu.VMEM((rows, many, span), F32),
            pltpu.VMEM((rows, many, span), BF16),
            pltpu.VMEM((shards, (stride - 8) * LAT // 128 + 8, 128), BF16),
            pltpu.SemaphoreType.DMA((rows, PARTS)),
            pltpu.SemaphoreType.DMA((2,)),
        ],
        compiler_params=pltpu.CompilerParams(vmem_limit_bytes=50 * 1024 * 1024),
        cost_estimate=pl.CostEstimate(
            flops=2 * rows * many * span * (width + LAT),
            bytes_accessed=keys.size * 2 + gathered.size * 4,
            transcendentals=rows * many * span,
        ),
        name="attend",
    )(lengths, gathered, keys)


def merge_kernel(offsets, got_ref, fresh_ref, fresh_lse_ref, *refs):
    *up_refs, out_ref, up = refs
    steps, rows, heads, _ = out_ref.shape
    shards = got_ref.shape[0]
    count = steps * rows * heads
    per_row = count // rows
    line = lax.axis_index("dp")
    chips = lax.axis_size("dp") // 2
    z = line // 2
    own = 1 - 2 * (line % 2)
    depth = up_refs[0].shape[2]
    spare = up_refs[1].shape[0] - 1

    def place(offset, block):
        chip = (z + own * offset + chips) % chips
        up[:, pl.ds(pl.multiple_of(chip * depth, depth), depth), :] = block

    for ref, mine, spans in zip(up_refs, (1, 1, -1, -1), offsets):
        for b, offset in enumerate(spans):
            place(mine * offset, ref[b])
    place(chips // 2, jnp.where(own < 0, up_refs[1][spare], up_refs[3][spare]))
    tail = got_ref[:, LAT // 128 * count :, :].astype(F32)
    sub = lax.broadcasted_iota(jnp.int32, (per_row, 128), 0)
    lane = lax.broadcasted_iota(jnp.int32, (per_row, 128), 1)
    eye = sub == lane

    def column(row):
        return jnp.sum(jnp.where(eye, row, 0.0), axis=1, keepdims=True)

    merged = []
    for r in range(rows):
        spread = tail[:, 3 * r] + tail[:, 3 * r + 1] + tail[:, 3 * r + 2]
        own = fresh_lse_ref[r : r + 1]
        top = jnp.maximum(jnp.max(spread, axis=0, keepdims=True), own)
        factor = jnp.exp(spread - top)
        own_factor = jnp.exp(own - top)
        scale = 1.0 / (jnp.sum(factor, axis=0, keepdims=True) + own_factor)
        factor = factor * scale
        first = r * per_row
        total = column(own_factor * scale) * fresh_ref[first : first + per_row]
        for d in range(shards):
            piece = jnp.concatenate(
                [
                    got_ref[d, lanes * per_row : (lanes + 1) * per_row, :]
                    for lanes in range(r * (LAT // 128), (r + 1) * (LAT // 128))
                ],
                axis=1,
            ).astype(F32)
            total += column(factor[d : d + 1]) * piece
        merged.append(total)
    latent = jnp.concatenate(merged, axis=0).astype(BF16)
    head = lax.broadcasted_iota(jnp.int32, (count, 128), 0) % heads
    result = jnp.zeros((count, 128), F32)
    for h in range(heads):
        product = jnp.dot(latent, up[h], preferred_element_type=F32)
        result = jnp.where(head == h, product, result)
    for r in range(rows):
        for s in range(steps):
            first = (r * steps + s) * heads
            out_ref[s, r] = result[first : first + heads]


def merge(got, fresh, fresh_lse, ups, offsets, steps, rows):
    _, heads, depth, width = ups[0].shape
    return pl.pallas_call(
        functools.partial(merge_kernel, offsets),
        out_shape=jax.ShapeDtypeStruct((steps, rows, heads, width), F32),
        in_specs=[vmem()] * (3 + len(ups)),
        out_specs=vmem(),
        scratch_shapes=[pltpu.VMEM((heads, LAT, width), BF16)],
        compiler_params=pltpu.CompilerParams(vmem_limit_bytes=16 * 1024 * 1024),
        name="merge",
    )(got, fresh, fresh_lse, *ups)


def body(queries, latent_cache, new_latent, lengths, value_up):
    steps, rows, heads, _ = queries.shape
    shards = lax.axis_size("ctx")
    lines = lax.axis_size("dp")
    chips = lines // 2

    def from_line(x, reach, cores=(0, 1)):
        pairs = []
        for line in range(lines):
            z, core = line // 2, line % 2
            if core in cores:
                pairs.append(((z + (1 - 2 * core) * reach) % chips * 2 + core, line))
        return lax.ppermute(x, "dp", pairs)

    def from_core(x):
        return lax.ppermute(x, "dp", [(i, i ^ 1) for i in range(lines)])

    packed = pack_queries(queries, shards)
    packed, value_up, lengths = lax.optimization_barrier((packed, value_up, lengths))
    gathered = lax.all_to_all(packed, "ctx", 0, 0, tiled=True)

    near = lax.all_gather(
        value_up, "dp", axis=1, tiled=True,
        axis_index_groups=[[2 * z, 2 * z + 1] for z in range(chips)],
    )[None]
    first = from_line(near, 4)

    fresh, fresh_lse = fresh_part(lengths, queries, new_latent)
    held = jnp.concatenate([near, first], axis=0)
    held, fresh, fresh_lse = lax.optimization_barrier((held, fresh, fresh_lse))
    second = from_line(held, 2)
    partial = attend(lengths, gathered, jnp.swapaxes(latent_cache, 1, 2))
    partial, second = lax.optimization_barrier((partial, second))
    got = lax.all_to_all(partial, "ctx", 0, 0, tiled=True)
    held = jnp.concatenate([held, second], axis=0)
    third = from_line(held, 1)
    eighth = from_line(second[-1:], 2, (1,))
    third, eighth = lax.optimization_barrier((third, eighth))
    third = jnp.concatenate([third, eighth], axis=0)
    ups = (held, third, from_core(held), from_core(third))
    even, odd = (0, 4, 2, 6), (1, 5, 3, 7)
    return merge(got, fresh, fresh_lse, ups, (even, odd, even, odd), steps, rows)


def solution(mesh):
    placed = (
        P(None, "dp", "ctx", None),
        P("dp", "ctx", None),
        P(None, "dp", None),
        P("dp"),
        P("ctx", "dp", None),
    )
    return jax.shard_map(
        body, mesh=mesh, in_specs=placed, out_specs=P(None, "dp", "ctx", None), check_vma=False
    )
```

```python
import functools

import jax
import jax.numpy as jnp
import numpy as np
from jax import lax
from jax.experimental import pallas as pl
from jax.experimental.pallas import tpu as pltpu
from jax.sharding import PartitionSpec as P

LAT = 512
ROPE = 64
HALF = 32
NOPE = 128
SCALE = (NOPE + ROPE) ** (-0.5)
LOG2E = 1.4426950408889634
FLOOR = -1e30
F32 = jnp.float32
BF16 = jnp.bfloat16
NT = (((1,), (1,)), ((), ()))


def vmem():
    return pl.BlockSpec(memory_space=pltpu.VMEM)


def smem():
    return pl.BlockSpec(memory_space=pltpu.SMEM)


def swap_halves(x):
    lane = lax.broadcasted_iota(jnp.int32, x.shape, x.ndim - 1)
    width = x.shape[-1]
    ahead = pltpu.roll(x, width - HALF, x.ndim - 1)
    behind = pltpu.roll(x, HALF, x.ndim - 1)
    return jnp.where(lane % ROPE < HALF, ahead, behind)


def pack_kernel(q_ref, out_ref):
    steps, rows, heads, _ = q_ref.shape
    parts = []
    rotary = []
    for r in range(rows):
        for s in range(steps):
            block = q_ref[s, r].astype(F32)
            parts.append(block[:, :LAT])
            rotary.append(block[:, LAT:])
    parts.append(jnp.concatenate(rotary, axis=1))
    whole = jnp.concatenate(parts, axis=0).astype(BF16)
    for d in range(out_ref.shape[0]):
        out_ref[d] = whole


def pack_queries(queries, shards):
    steps, rows, heads, _ = queries.shape
    count = steps * rows * heads
    return pl.pallas_call(
        pack_kernel,
        out_shape=jax.ShapeDtypeStruct((shards, count + heads, LAT), BF16),
        in_specs=[vmem()],
        out_specs=vmem(),
        name="pack_queries",
    )(queries)


def rotation(lengths_ref, steps, shape, step_of, row_of):
    row = lax.broadcasted_iota(jnp.int32, shape, 0)
    lane = lax.broadcasted_iota(jnp.int32, shape, 1)
    which = row_of(row)
    position = jnp.zeros(shape, jnp.int32)
    for r in range(lengths_ref.shape[0]):
        position = jnp.where(which == r, lengths_ref[r], position)
    position += step_of(row, lane)
    frequency = jnp.zeros(shape, F32)
    for i in range(HALF):
        value = float(np.float32(10000.0 ** (-2.0 * i / ROPE)))
        frequency = jnp.where(lane % HALF == i, value, frequency)
    angle = position.astype(F32) * frequency
    sine = jnp.sin(angle)
    return jnp.cos(angle), jnp.where(lane % ROPE < HALF, -sine, sine)


def fresh_kernel(lengths_ref, q_ref, new_ref, mixed_ref, lse_ref):
    steps, rows, heads, _ = q_ref.shape
    count = rows * steps * heads
    keys = rows * steps
    cos, sin = rotation(
        lengths_ref, steps, (keys, 2 * ROPE), lambda row, _: row % steps, lambda row: row // steps
    )
    q_lat = []
    q_rot = []
    key_lat = []
    key_rot = []
    for r in range(rows):
        for s in range(steps):
            row_cos = cos[r * steps + s : r * steps + s + 1]
            row_sin = sin[r * steps + s : r * steps + s + 1]
            block = q_ref[s, r].astype(F32)
            q_lat.append(block[:, :LAT])
            wide = jnp.concatenate([block[:, LAT:], block[:, LAT:]], axis=1)
            q_rot.append(wide * row_cos + swap_halves(wide) * row_sin)
            key = new_ref[s, r : r + 1].astype(F32)
            key_lat.append(key[:, :LAT])
            wide = jnp.concatenate([key[:, LAT:], key[:, LAT:]], axis=1)
            wide = jnp.broadcast_to(wide, (8, 2 * ROPE))
            wide = wide * row_cos + swap_halves(wide) * row_sin
            key_rot.append(wide[:1])
    q_lat = jnp.concatenate(q_lat, axis=0).astype(BF16)
    q_rot = jnp.concatenate(q_rot, axis=0)[:, :ROPE].astype(BF16)
    pad = jnp.zeros((128 - keys, LAT), F32)
    key_lat = jnp.concatenate(key_lat + [pad], axis=0).astype(BF16)
    key_rot = jnp.concatenate(key_rot + [pad[:, : 2 * ROPE]], axis=0)[:, :ROPE].astype(BF16)
    scores = lax.dot_general(q_lat, key_lat, NT, preferred_element_type=F32)
    scores += lax.dot_general(q_rot, key_rot, NT, preferred_element_type=F32)
    scores *= SCALE
    query = lax.broadcasted_iota(jnp.int32, (count, 128), 0) // heads
    key = lax.broadcasted_iota(jnp.int32, (count, 128), 1)
    valid = (key <= query) & (key // steps == query // steps)
    scores = jnp.where(valid, scores, FLOOR)
    top = jnp.max(scores, axis=1, keepdims=True)
    weights = jnp.where(valid, jnp.exp(scores - top), 0.0)
    total = jnp.sum(weights, axis=1, keepdims=True)
    mixed = jnp.dot(weights.astype(BF16), key_lat, preferred_element_type=F32)
    mixed_ref[...] = mixed / total
    lse_ref[...] = as_rows((top + jnp.log(total)).reshape(rows, steps * heads, 1))


def as_rows(column):
    n, span, _ = column.shape
    row = lax.broadcasted_iota(jnp.int32, (n, span, 128), 1)
    lane = lax.broadcasted_iota(jnp.int32, (n, span, 128), 2)
    return jnp.sum(jnp.where(row == lane, column, 0.0), axis=1)


def fresh_part(lengths, queries, new_latent):
    steps, rows, heads, _ = queries.shape
    count = steps * rows * heads
    return pl.pallas_call(
        fresh_kernel,
        out_shape=(
            jax.ShapeDtypeStruct((count, LAT), F32),
            jax.ShapeDtypeStruct((rows, 128), F32),
        ),
        in_specs=[smem()] + [vmem()] * 2,
        out_specs=(vmem(),) * 2,
        name="fresh_part",
    )(lengths, queries, new_latent)


CHUNK = 512
PARTS = 2


def attend_kernel(lengths_ref, q_ref, cache_ref, out_hbm, *scratch):
    keys_ref, q_scr, s_scr, p_scr, out_ref, sems, out_sems = scratch
    rows, width, span = cache_ref.shape
    shards, stride, _ = q_ref.shape
    heads = 8
    count = stride - heads
    per_row = count // rows
    steps = per_row // heads
    many = shards * per_row
    deep = width // PARTS
    copies = [
        [
            pltpu.make_async_copy(
                cache_ref.at[r, pl.ds(part * 256, 256 + 64 * part)],
                keys_ref.at[r, pl.ds(part * 256, 256 + 64 * part)],
                sems.at[r, part],
            )
            for part in range(PARTS)
        ]
        for r in range(rows)
    ]
    for copy in copies[0]:
        copy.start()
    packed = q_ref[:, count:, :].astype(F32).reshape(shards * heads, LAT)
    first_slot = lax.axis_index("ctx") * span
    pad = keys_ref.shape[1] - width
    cos, sin = rotation(
        lengths_ref, steps, (8, steps * ROPE), lambda _, lane: lane // ROPE, lambda row: row
    )
    for r in range(rows):
        live = lengths_ref[r] - first_slot
        slot = lax.broadcasted_iota(jnp.int32, (pad, span), 1)
        line = lax.broadcasted_iota(jnp.int32, (pad, span), 0)
        keys_ref[r, width:, :] = jnp.where((line == 0) & (slot >= live), FLOOR, 0.0).astype(BF16)
        q_scr[r, :, :LAT] = q_ref[:, r * per_row : (r + 1) * per_row, :].reshape(many, LAT)
        part = packed[:, r * steps * ROPE : (r + 1) * steps * ROPE]
        turned = part * cos[r : r + 1] + swap_halves(part) * sin[r : r + 1]
        turned = jnp.stack(
            [
                turned[:, s * ROPE : (s + 1) * ROPE].reshape(shards, heads, ROPE)
                for s in range(steps)
            ],
            axis=1,
        ).reshape(many, ROPE)
        lane = lax.broadcasted_iota(jnp.int32, (many, pad), 1)
        one = jnp.where(lane == 0, 1.0, 0.0)
        q_scr[r, :, LAT:] = jnp.concatenate([turned, one], axis=1).astype(BF16)

    half = LAT // 128 * per_row
    outs = [
        pltpu.make_async_copy(out_ref.at[:, pl.ds(0, half)], out_hbm.at[:, pl.ds(0, half)], out_sems.at[0]),
        pltpu.make_async_copy(
            out_ref.at[:, pl.ds(half, out_hbm.shape[1] - half)],
            out_hbm.at[:, pl.ds(half, out_hbm.shape[1] - half)],
            out_sems.at[1],
        ),
    ]

    def partial_score(r, lo, hi, fresh):
        for first in range(0, span, CHUNK):
            part = jnp.dot(
                q_scr[r, :, lo:hi], keys_ref[r, lo:hi, first : first + CHUNK], preferred_element_type=F32
            )
            if not fresh:
                part += s_scr[r, :, first : first + CHUNK]
            s_scr[r, :, first : first + CHUNK] = part

    def score(r, first, top):
        if r == 0:
            part = s_scr[r, :, first : first + CHUNK]
            part += jnp.dot(q_scr[r, :, 256:], keys_ref[r, 256:, first : first + CHUNK], preferred_element_type=F32)
        else:
            part = jnp.dot(
                q_scr[r], keys_ref[r, :, first : first + CHUNK], preferred_element_type=F32
            )
        s_scr[r, :, first : first + CHUNK] = part
        for lanes in range(0, CHUNK, 128):
            block = part[:, lanes : lanes + 128]
            top = block if top is None else jnp.maximum(top, block)
        return top

    def weigh(r, first, level, total):
        part = jnp.exp2((s_scr[r, :, first : first + CHUNK] - level) * (SCALE * LOG2E))
        p_scr[r, :, first : first + CHUNK] = part.astype(BF16)
        for lanes in range(0, CHUNK, 128):
            block = part[:, lanes : lanes + 128]
            total = block if total is None else total + block
        return total

    def mix(r):
        return lax.dot_general(p_scr[r], keys_ref[r, :LAT, :], NT, preferred_element_type=F32)

    def finish(r, level, total, mixed):
        total = jnp.sum(total, axis=1, keepdims=True)
        mixed = (mixed * (1.0 / total)).astype(BF16).reshape(shards, per_row, LAT)
        for lanes in range(LAT // 128):
            first = (r * (LAT // 128) + lanes) * per_row
            out_ref[:, first : first + per_row, :] = mixed[:, :, lanes * 128 : (lanes + 1) * 128]
        if r == 0:
            outs[0].start()
        lse = jnp.where(lengths_ref[r] > first_slot, level * SCALE + jnp.log(total), FLOOR)
        return as_rows(lse.reshape(shards, per_row, 1))

    levels = []
    totals = [None] * rows
    for r in range(rows):
        copies[r][0].wait()
        if r == 0:
            partial_score(0, 0, 256, True)
        copies[r][1].wait()
        if r + 1 < rows:
            for copy in copies[r + 1]:
                copy.start()
        top = None
        for first in range(0, span, CHUNK):
            top = score(r, first, top)
        levels.append(jnp.max(top, axis=1, keepdims=True))
        if r == 0:
            for first in range(0, span, CHUNK):
                totals[0] = weigh(0, first, levels[0], totals[0])
    lse_rows = []
    for r in range(rows):
        mixed = mix(r)
        if r == rows - 2:
            for first in range(0, span, CHUNK):
                totals[r + 1] = weigh(r + 1, first, levels[r + 1], totals[r + 1])
        lse_rows.append(finish(r, levels[r], totals[r], mixed))
    tail = jnp.zeros((shards, heads, 128), F32)
    which = lax.broadcasted_iota(jnp.int32, tail.shape, 1)
    for r in range(rows):
        rest = lse_rows[r]
        for term in range(3):
            piece = rest.astype(BF16).astype(F32)
            tail = jnp.where(which == 3 * r + term, piece[:, None, :], tail)
            rest = rest - piece
    out_ref[:, LAT // 128 * count :, :] = tail.astype(BF16)
    outs[1].start()
    for out in outs:
        out.wait()


def attend(lengths, gathered, keys):
    rows, width, span = keys.shape
    shards, stride, _ = gathered.shape
    many = (stride - 8) // rows * shards
    padded = width + 64
    return pl.pallas_call(
        attend_kernel,
        out_shape=jax.ShapeDtypeStruct((shards, (stride - 8) * LAT // 128 + 8, 128), BF16),
        in_specs=[smem(), vmem(), pl.BlockSpec(memory_space=pltpu.HBM)],
        out_specs=pl.BlockSpec(memory_space=pltpu.HBM),
        scratch_shapes=[
            pltpu.VMEM((rows, padded, span), BF16),
            pltpu.VMEM((rows, many, padded), BF16),
            pltpu.VMEM((rows, many, span), F32),
            pltpu.VMEM((rows, many, span), BF16),
            pltpu.VMEM((shards, (stride - 8) * LAT // 128 + 8, 128), BF16),
            pltpu.SemaphoreType.DMA((rows, PARTS)),
            pltpu.SemaphoreType.DMA((2,)),
        ],
        compiler_params=pltpu.CompilerParams(vmem_limit_bytes=50 * 1024 * 1024),
        cost_estimate=pl.CostEstimate(
            flops=2 * rows * many * span * (width + LAT),
            bytes_accessed=keys.size * 2 + gathered.size * 4,
            transcendentals=rows * many * span,
        ),
        name="attend",
    )(lengths, gathered, keys)


def merge_kernel(offsets, got_ref, fresh_ref, fresh_lse_ref, *refs):
    *up_refs, out_ref, up = refs
    steps, rows, heads, _ = out_ref.shape
    shards = got_ref.shape[0]
    count = steps * rows * heads
    per_row = count // rows
    line = lax.axis_index("dp")
    chips = lax.axis_size("dp") // 2
    z = line // 2
    own = 1 - 2 * (line % 2)
    depth = up_refs[0].shape[2]
    spare = up_refs[1].shape[0] - 1

    def place(offset, block):
        chip = (z + own * offset + chips) % chips
        up[:, pl.ds(pl.multiple_of(chip * depth, depth), depth), :] = block

    for ref, mine, spans in zip(up_refs, (1, 1, -1, -1), offsets):
        for b, offset in enumerate(spans):
            place(mine * offset, ref[b])
    place(chips // 2, jnp.where(own < 0, up_refs[1][spare], up_refs[3][spare]))
    tail = got_ref[:, LAT // 128 * count :, :].astype(F32)
    sub = lax.broadcasted_iota(jnp.int32, (per_row, 128), 0)
    lane = lax.broadcasted_iota(jnp.int32, (per_row, 128), 1)
    eye = sub == lane

    def column(row):
        return jnp.sum(jnp.where(eye, row, 0.0), axis=1, keepdims=True)

    merged = []
    for r in range(rows):
        spread = tail[:, 3 * r] + tail[:, 3 * r + 1] + tail[:, 3 * r + 2]
        own = fresh_lse_ref[r : r + 1]
        top = jnp.maximum(jnp.max(spread, axis=0, keepdims=True), own)
        factor = jnp.exp(spread - top)
        own_factor = jnp.exp(own - top)
        scale = 1.0 / (jnp.sum(factor, axis=0, keepdims=True) + own_factor)
        factor = factor * scale
        first = r * per_row
        total = column(own_factor * scale) * fresh_ref[first : first + per_row]
        for d in range(shards):
            piece = jnp.concatenate(
                [
                    got_ref[d, lanes * per_row : (lanes + 1) * per_row, :]
                    for lanes in range(r * (LAT // 128), (r + 1) * (LAT // 128))
                ],
                axis=1,
            ).astype(F32)
            total += column(factor[d : d + 1]) * piece
        merged.append(total)
    latent = jnp.concatenate(merged, axis=0).astype(BF16)
    head = lax.broadcasted_iota(jnp.int32, (count, 128), 0) % heads
    result = jnp.zeros((count, 128), F32)
    for h in range(heads):
        product = jnp.dot(latent, up[h], preferred_element_type=F32)
        result = jnp.where(head == h, product, result)
    for r in range(rows):
        for s in range(steps):
            first = (r * steps + s) * heads
            out_ref[s, r] = result[first : first + heads]


def merge(got, fresh, fresh_lse, ups, offsets, steps, rows):
    _, heads, depth, width = ups[0].shape
    return pl.pallas_call(
        functools.partial(merge_kernel, offsets),
        out_shape=jax.ShapeDtypeStruct((steps, rows, heads, width), F32),
        in_specs=[vmem()] * (3 + len(ups)),
        out_specs=vmem(),
        scratch_shapes=[pltpu.VMEM((heads, LAT, width), BF16)],
        compiler_params=pltpu.CompilerParams(vmem_limit_bytes=16 * 1024 * 1024),
        name="merge",
    )(got, fresh, fresh_lse, *ups)


def body(queries, latent_cache, new_latent, lengths, value_up):
    steps, rows, heads, _ = queries.shape
    shards = lax.axis_size("ctx")
    lines = lax.axis_size("dp")
    chips = lines // 2

    def from_line(x, reach, cores=(0, 1)):
        pairs = []
        for line in range(lines):
            z, core = line // 2, line % 2
            if core in cores:
                pairs.append(((z + (1 - 2 * core) * reach) % chips * 2 + core, line))
        return lax.ppermute(x, "dp", pairs)

    def from_core(x):
        return lax.ppermute(x, "dp", [(i, i ^ 1) for i in range(lines)])

    packed = pack_queries(queries, shards)
    packed, value_up, lengths = lax.optimization_barrier((packed, value_up, lengths))
    gathered = lax.all_to_all(packed, "ctx", 0, 0, tiled=True)

    near = lax.all_gather(
        value_up, "dp", axis=1, tiled=True,
        axis_index_groups=[[2 * z, 2 * z + 1] for z in range(chips)],
    )[None]
    first = from_line(near, 4)

    fresh, fresh_lse = fresh_part(lengths, queries, new_latent)
    held = jnp.concatenate([near, first], axis=0)
    held, fresh, fresh_lse = lax.optimization_barrier((held, fresh, fresh_lse))
    second = from_line(held, 2)
    partial = attend(lengths, gathered, jnp.swapaxes(latent_cache, 1, 2))
    partial, second = lax.optimization_barrier((partial, second))
    got = lax.all_to_all(partial, "ctx", 0, 0, tiled=True)
    held = jnp.concatenate([held, second], axis=0)
    third = from_line(held, 1)
    eighth = from_line(second[-1:], 2, (1,))
    eighth, held = lax.optimization_barrier((eighth, held))
    third, eighth, other = lax.optimization_barrier((third, eighth, from_core(held)))
    third = jnp.concatenate([third, eighth], axis=0)
    ups = (held, third, other, from_core(third))
    even, odd = (0, 4, 2, 6), (1, 5, 3, 7)
    return merge(got, fresh, fresh_lse, ups, (even, odd, even, odd), steps, rows)


def solution(mesh):
    placed = (
        P(None, "dp", "ctx", None),
        P("dp", "ctx", None),
        P(None, "dp", None),
        P("dp"),
        P("ctx", "dp", None),
    )
    return jax.shard_map(
        body, mesh=mesh, in_specs=placed, out_specs=P(None, "dp", "ctx", None), check_vma=False
    )
```

```python
import functools

import jax
import jax.numpy as jnp
import numpy as np
from jax import lax
from jax.experimental import pallas as pl
from jax.experimental.pallas import tpu as pltpu
from jax.sharding import PartitionSpec as P

LAT = 512
ROPE = 64
HALF = 32
NOPE = 128
SCALE = (NOPE + ROPE) ** (-0.5)
LOG2E = 1.4426950408889634
FLOOR = -1e30
F32 = jnp.float32
BF16 = jnp.bfloat16
NT = (((1,), (1,)), ((), ()))


def vmem():
    return pl.BlockSpec(memory_space=pltpu.VMEM)


def smem():
    return pl.BlockSpec(memory_space=pltpu.SMEM)


def swap_halves(x):
    lane = lax.broadcasted_iota(jnp.int32, x.shape, x.ndim - 1)
    width = x.shape[-1]
    ahead = pltpu.roll(x, width - HALF, x.ndim - 1)
    behind = pltpu.roll(x, HALF, x.ndim - 1)
    return jnp.where(lane % ROPE < HALF, ahead, behind)


def pack_kernel(q_ref, out_ref):
    steps, rows, heads, _ = q_ref.shape
    parts = []
    rotary = []
    for r in range(rows):
        for s in range(steps):
            block = q_ref[s, r].astype(F32)
            parts.append(block[:, :LAT])
            rotary.append(block[:, LAT:])
    parts.append(jnp.concatenate(rotary, axis=1))
    whole = jnp.concatenate(parts, axis=0).astype(BF16)
    for d in range(out_ref.shape[0]):
        out_ref[d] = whole


def pack_queries(queries, shards):
    steps, rows, heads, _ = queries.shape
    count = steps * rows * heads
    return pl.pallas_call(
        pack_kernel,
        out_shape=jax.ShapeDtypeStruct((shards, count + heads, LAT), BF16),
        in_specs=[vmem()],
        out_specs=vmem(),
        name="pack_queries",
    )(queries)


def rotation(lengths_ref, steps, shape, step_of, row_of):
    row = lax.broadcasted_iota(jnp.int32, shape, 0)
    lane = lax.broadcasted_iota(jnp.int32, shape, 1)
    which = row_of(row)
    position = jnp.zeros(shape, jnp.int32)
    for r in range(lengths_ref.shape[0]):
        position = jnp.where(which == r, lengths_ref[r], position)
    position += step_of(row, lane)
    frequency = jnp.zeros(shape, F32)
    for i in range(HALF):
        value = float(np.float32(10000.0 ** (-2.0 * i / ROPE)))
        frequency = jnp.where(lane % HALF == i, value, frequency)
    angle = position.astype(F32) * frequency
    sine = jnp.sin(angle)
    return jnp.cos(angle), jnp.where(lane % ROPE < HALF, -sine, sine)


def fresh_kernel(lengths_ref, q_ref, new_ref, mixed_ref, lse_ref):
    steps, rows, heads, _ = q_ref.shape
    count = rows * steps * heads
    keys = rows * steps
    cos, sin = rotation(
        lengths_ref, steps, (keys, 2 * ROPE), lambda row, _: row % steps, lambda row: row // steps
    )
    q_lat = []
    q_rot = []
    key_lat = []
    key_rot = []
    for r in range(rows):
        for s in range(steps):
            row_cos = cos[r * steps + s : r * steps + s + 1]
            row_sin = sin[r * steps + s : r * steps + s + 1]
            block = q_ref[s, r].astype(F32)
            q_lat.append(block[:, :LAT])
            wide = jnp.concatenate([block[:, LAT:], block[:, LAT:]], axis=1)
            q_rot.append(wide * row_cos + swap_halves(wide) * row_sin)
            key = new_ref[s, r : r + 1].astype(F32)
            key_lat.append(key[:, :LAT])
            wide = jnp.concatenate([key[:, LAT:], key[:, LAT:]], axis=1)
            wide = jnp.broadcast_to(wide, (8, 2 * ROPE))
            wide = wide * row_cos + swap_halves(wide) * row_sin
            key_rot.append(wide[:1])
    q_lat = jnp.concatenate(q_lat, axis=0).astype(BF16)
    q_rot = jnp.concatenate(q_rot, axis=0)[:, :ROPE].astype(BF16)
    pad = jnp.zeros((128 - keys, LAT), F32)
    key_lat = jnp.concatenate(key_lat + [pad], axis=0).astype(BF16)
    key_rot = jnp.concatenate(key_rot + [pad[:, : 2 * ROPE]], axis=0)[:, :ROPE].astype(BF16)
    scores = lax.dot_general(q_lat, key_lat, NT, preferred_element_type=F32)
    scores += lax.dot_general(q_rot, key_rot, NT, preferred_element_type=F32)
    scores *= SCALE
    query = lax.broadcasted_iota(jnp.int32, (count, 128), 0) // heads
    key = lax.broadcasted_iota(jnp.int32, (count, 128), 1)
    valid = (key <= query) & (key // steps == query // steps)
    scores = jnp.where(valid, scores, FLOOR)
    top = jnp.max(scores, axis=1, keepdims=True)
    weights = jnp.where(valid, jnp.exp(scores - top), 0.0)
    total = jnp.sum(weights, axis=1, keepdims=True)
    mixed = jnp.dot(weights.astype(BF16), key_lat, preferred_element_type=F32)
    mixed_ref[...] = mixed / total
    lse_ref[...] = as_rows((top + jnp.log(total)).reshape(rows, steps * heads, 1))


def as_rows(column):
    n, span, _ = column.shape
    row = lax.broadcasted_iota(jnp.int32, (n, span, 128), 1)
    lane = lax.broadcasted_iota(jnp.int32, (n, span, 128), 2)
    return jnp.sum(jnp.where(row == lane, column, 0.0), axis=1)


def fresh_part(lengths, queries, new_latent):
    steps, rows, heads, _ = queries.shape
    count = steps * rows * heads
    return pl.pallas_call(
        fresh_kernel,
        out_shape=(
            jax.ShapeDtypeStruct((count, LAT), F32),
            jax.ShapeDtypeStruct((rows, 128), F32),
        ),
        in_specs=[smem()] + [vmem()] * 2,
        out_specs=(vmem(),) * 2,
        name="fresh_part",
    )(lengths, queries, new_latent)


CHUNK = 512
PARTS = 2


def attend_kernel(lengths_ref, q_ref, cache_ref, out_hbm, *scratch):
    keys_ref, q_scr, s_scr, p_scr, out_ref, sems, out_sems = scratch
    rows, width, span = cache_ref.shape
    shards, stride, _ = q_ref.shape
    heads = 8
    count = stride - heads
    per_row = count // rows
    steps = per_row // heads
    many = shards * per_row
    deep = width // PARTS
    copies = [
        [
            pltpu.make_async_copy(
                cache_ref.at[r, pl.ds(part * 256, 256 + 64 * part)],
                keys_ref.at[r, pl.ds(part * 256, 256 + 64 * part)],
                sems.at[r, part],
            )
            for part in range(PARTS)
        ]
        for r in range(rows)
    ]
    for copy in copies[0]:
        copy.start()
    packed = q_ref[:, count:, :].astype(F32).reshape(shards * heads, LAT)
    first_slot = lax.axis_index("ctx") * span
    pad = keys_ref.shape[1] - width
    cos, sin = rotation(
        lengths_ref, steps, (8, steps * ROPE), lambda _, lane: lane // ROPE, lambda row: row
    )
    for r in range(rows):
        live = lengths_ref[r] - first_slot
        slot = lax.broadcasted_iota(jnp.int32, (pad, span), 1)
        line = lax.broadcasted_iota(jnp.int32, (pad, span), 0)
        keys_ref[r, width:, :] = jnp.where((line == 0) & (slot >= live), FLOOR, 0.0).astype(BF16)
        q_scr[r, :, :LAT] = q_ref[:, r * per_row : (r + 1) * per_row, :].reshape(many, LAT)
        part = packed[:, r * steps * ROPE : (r + 1) * steps * ROPE]
        turned = part * cos[r : r + 1] + swap_halves(part) * sin[r : r + 1]
        turned = jnp.stack(
            [
                turned[:, s * ROPE : (s + 1) * ROPE].reshape(shards, heads, ROPE)
                for s in range(steps)
            ],
            axis=1,
        ).reshape(many, ROPE)
        lane = lax.broadcasted_iota(jnp.int32, (many, pad), 1)
        one = jnp.where(lane == 0, 1.0, 0.0)
        q_scr[r, :, LAT:] = jnp.concatenate([turned, one], axis=1).astype(BF16)

    half = LAT // 128 * per_row
    outs = [
        pltpu.make_async_copy(out_ref.at[:, pl.ds(0, half)], out_hbm.at[:, pl.ds(0, half)], out_sems.at[0]),
        pltpu.make_async_copy(
            out_ref.at[:, pl.ds(half, out_hbm.shape[1] - half)],
            out_hbm.at[:, pl.ds(half, out_hbm.shape[1] - half)],
            out_sems.at[1],
        ),
    ]

    def partial_score(r, lo, hi, fresh):
        for first in range(0, span, CHUNK):
            part = jnp.dot(
                q_scr[r, :, lo:hi], keys_ref[r, lo:hi, first : first + CHUNK], preferred_element_type=F32
            )
            if not fresh:
                part += s_scr[r, :, first : first + CHUNK]
            s_scr[r, :, first : first + CHUNK] = part

    def score(r, first, top):
        if r == 0:
            part = s_scr[r, :, first : first + CHUNK]
            part += jnp.dot(q_scr[r, :, 256:], keys_ref[r, 256:, first : first + CHUNK], preferred_element_type=F32)
        else:
            part = jnp.dot(
                q_scr[r], keys_ref[r, :, first : first + CHUNK], preferred_element_type=F32
            )
        s_scr[r, :, first : first + CHUNK] = part
        for lanes in range(0, CHUNK, 128):
            block = part[:, lanes : lanes + 128]
            top = block if top is None else jnp.maximum(top, block)
        return top

    def weigh(r, first, level, total):
        part = jnp.exp2((s_scr[r, :, first : first + CHUNK] - level) * (SCALE * LOG2E))
        p_scr[r, :, first : first + CHUNK] = part.astype(BF16)
        for lanes in range(0, CHUNK, 128):
            block = part[:, lanes : lanes + 128]
            total = block if total is None else total + block
        return total

    def mix(r):
        return lax.dot_general(p_scr[r], keys_ref[r, :LAT, :], NT, preferred_element_type=F32)

    def finish(r, level, total, mixed):
        total = jnp.sum(total, axis=1, keepdims=True)
        mixed = (mixed * (1.0 / total)).astype(BF16).reshape(shards, per_row, LAT)
        for lanes in range(LAT // 128):
            first = (r * (LAT // 128) + lanes) * per_row
            out_ref[:, first : first + per_row, :] = mixed[:, :, lanes * 128 : (lanes + 1) * 128]
        if r == 0:
            outs[0].start()
        lse = jnp.where(lengths_ref[r] > first_slot, level * SCALE + jnp.log(total), FLOOR)
        return as_rows(lse.reshape(shards, per_row, 1))

    levels = []
    totals = [None] * rows
    for r in range(rows):
        copies[r][0].wait()
        if r == 0:
            copies[1][0].start()
            partial_score(0, 0, 256, True)
        copies[r][1].wait()
        if r == 0:
            copies[1][1].start()
        top = None
        for first in range(0, span, CHUNK):
            top = score(r, first, top)
        levels.append(jnp.max(top, axis=1, keepdims=True))
        if r == 0:
            for first in range(0, span, CHUNK):
                totals[0] = weigh(0, first, levels[0], totals[0])
    lse_rows = []
    for r in range(rows):
        mixed = mix(r)
        if r == rows - 2:
            for first in range(0, span, CHUNK):
                totals[r + 1] = weigh(r + 1, first, levels[r + 1], totals[r + 1])
        lse_rows.append(finish(r, levels[r], totals[r], mixed))
    tail = jnp.zeros((shards, heads, 128), F32)
    which = lax.broadcasted_iota(jnp.int32, tail.shape, 1)
    for r in range(rows):
        rest = lse_rows[r]
        for term in range(3):
            piece = rest.astype(BF16).astype(F32)
            tail = jnp.where(which == 3 * r + term, piece[:, None, :], tail)
            rest = rest - piece
    out_ref[:, LAT // 128 * count :, :] = tail.astype(BF16)
    outs[1].start()
    for out in outs:
        out.wait()


def attend(lengths, gathered, keys):
    rows, width, span = keys.shape
    shards, stride, _ = gathered.shape
    many = (stride - 8) // rows * shards
    padded = width + 64
    return pl.pallas_call(
        attend_kernel,
        out_shape=jax.ShapeDtypeStruct((shards, (stride - 8) * LAT // 128 + 8, 128), BF16),
        in_specs=[smem(), vmem(), pl.BlockSpec(memory_space=pltpu.HBM)],
        out_specs=pl.BlockSpec(memory_space=pltpu.HBM),
        scratch_shapes=[
            pltpu.VMEM((rows, padded, span), BF16),
            pltpu.VMEM((rows, many, padded), BF16),
            pltpu.VMEM((rows, many, span), F32),
            pltpu.VMEM((rows, many, span), BF16),
            pltpu.VMEM((shards, (stride - 8) * LAT // 128 + 8, 128), BF16),
            pltpu.SemaphoreType.DMA((rows, PARTS)),
            pltpu.SemaphoreType.DMA((2,)),
        ],
        compiler_params=pltpu.CompilerParams(vmem_limit_bytes=50 * 1024 * 1024),
        cost_estimate=pl.CostEstimate(
            flops=2 * rows * many * span * (width + LAT),
            bytes_accessed=keys.size * 2 + gathered.size * 4,
            transcendentals=rows * many * span,
        ),
        name="attend",
    )(lengths, gathered, keys)


def merge_kernel(offsets, got_ref, fresh_ref, fresh_lse_ref, *refs):
    *up_refs, out_ref, up = refs
    steps, rows, heads, _ = out_ref.shape
    shards = got_ref.shape[0]
    count = steps * rows * heads
    per_row = count // rows
    line = lax.axis_index("dp")
    chips = lax.axis_size("dp") // 2
    z = line // 2
    own = 1 - 2 * (line % 2)
    depth = up_refs[0].shape[2]
    spare = up_refs[1].shape[0] - 1

    def place(offset, block):
        chip = (z + own * offset + chips) % chips
        lines = pl.ds(pl.multiple_of(chip * depth, depth), depth)
        for h in range(heads):
            up[h // 2, lines, h % 2 * 128 : h % 2 * 128 + 128] = block[h]

    for ref, mine, spans in zip(up_refs, (1, 1, -1, -1), offsets):
        for b, offset in enumerate(spans):
            place(mine * offset, ref[b])
    place(chips // 2, jnp.where(own < 0, up_refs[1][spare], up_refs[3][spare]))
    tail = got_ref[:, LAT // 128 * count :, :].astype(F32)
    sub = lax.broadcasted_iota(jnp.int32, (per_row, 128), 0)
    lane = lax.broadcasted_iota(jnp.int32, (per_row, 128), 1)
    eye = sub == lane

    def column(row):
        return jnp.sum(jnp.where(eye, row, 0.0), axis=1, keepdims=True)

    merged = []
    for r in range(rows):
        spread = tail[:, 3 * r] + tail[:, 3 * r + 1] + tail[:, 3 * r + 2]
        own = fresh_lse_ref[r : r + 1]
        top = jnp.maximum(jnp.max(spread, axis=0, keepdims=True), own)
        factor = jnp.exp(spread - top)
        own_factor = jnp.exp(own - top)
        scale = 1.0 / (jnp.sum(factor, axis=0, keepdims=True) + own_factor)
        factor = factor * scale
        first = r * per_row
        total = column(own_factor * scale) * fresh_ref[first : first + per_row]
        for d in range(shards):
            piece = jnp.concatenate(
                [
                    got_ref[d, lanes * per_row : (lanes + 1) * per_row, :]
                    for lanes in range(r * (LAT // 128), (r + 1) * (LAT // 128))
                ],
                axis=1,
            ).astype(F32)
            total += column(factor[d : d + 1]) * piece
        merged.append(total)
    latent = jnp.concatenate(merged, axis=0).astype(BF16)
    head = lax.broadcasted_iota(jnp.int32, (count, 128), 0) % heads
    result = jnp.zeros((count, 128), F32)
    for h in range(0, heads, 2):
        product = jnp.dot(latent, up[h // 2], preferred_element_type=F32)
        result = jnp.where(head == h, product[:, :128], result)
        result = jnp.where(head == h + 1, product[:, 128:], result)
    for r in range(rows):
        for s in range(steps):
            first = (r * steps + s) * heads
            out_ref[s, r] = result[first : first + heads]


def merge(got, fresh, fresh_lse, ups, offsets, steps, rows):
    _, heads, depth, width = ups[0].shape
    return pl.pallas_call(
        functools.partial(merge_kernel, offsets),
        out_shape=jax.ShapeDtypeStruct((steps, rows, heads, width), F32),
        in_specs=[vmem()] * (3 + len(ups)),
        out_specs=vmem(),
        scratch_shapes=[pltpu.VMEM((heads // 2, LAT, 2 * width), BF16)],
        compiler_params=pltpu.CompilerParams(vmem_limit_bytes=16 * 1024 * 1024),
        name="merge",
    )(got, fresh, fresh_lse, *ups)


def body(queries, latent_cache, new_latent, lengths, value_up):
    steps, rows, heads, _ = queries.shape
    shards = lax.axis_size("ctx")
    lines = lax.axis_size("dp")
    chips = lines // 2

    def from_line(x, reach, cores=(0, 1)):
        pairs = []
        for line in range(lines):
            z, core = line // 2, line % 2
            if core in cores:
                pairs.append(((z + (1 - 2 * core) * reach) % chips * 2 + core, line))
        return lax.ppermute(x, "dp", pairs)

    def from_core(x):
        return lax.ppermute(x, "dp", [(i, i ^ 1) for i in range(lines)])

    packed = pack_queries(queries, shards)
    packed, value_up, lengths = lax.optimization_barrier((packed, value_up, lengths))
    gathered = lax.all_to_all(packed, "ctx", 0, 0, tiled=True)

    near = lax.all_gather(
        value_up, "dp", axis=1, tiled=True,
        axis_index_groups=[[2 * z, 2 * z + 1] for z in range(chips)],
    )[None]
    first = from_line(near, 4)

    fresh, fresh_lse = fresh_part(lengths, queries, new_latent)
    held = jnp.concatenate([near, first], axis=0)
    held, fresh, fresh_lse = lax.optimization_barrier((held, fresh, fresh_lse))
    second = from_line(held, 2)
    partial = attend(lengths, gathered, jnp.swapaxes(latent_cache, 1, 2))
    partial, second = lax.optimization_barrier((partial, second))
    got = lax.all_to_all(partial, "ctx", 0, 0, tiled=True)
    held = jnp.concatenate([held, second], axis=0)
    third = from_line(held, 1)
    eighth = from_line(second[-1:], 2, (1,))
    eighth, held = lax.optimization_barrier((eighth, held))
    third, eighth, other = lax.optimization_barrier((third, eighth, from_core(held)))
    third = jnp.concatenate([third, eighth], axis=0)
    ups = (held, third, other, from_core(third))
    even, odd = (0, 4, 2, 6), (1, 5, 3, 7)
    return merge(got, fresh, fresh_lse, ups, (even, odd, even, odd), steps, rows)


def solution(mesh):
    placed = (
        P(None, "dp", "ctx", None),
        P("dp", "ctx", None),
        P(None, "dp", None),
        P("dp"),
        P("ctx", "dp", None),
    )
    return jax.shard_map(
        body, mesh=mesh, in_specs=placed, out_specs=P(None, "dp", "ctx", None), check_vma=False
    )
```
